256 devices in a mesh: dp: 16 (over z, core), expert: 16 (over y, x).
Axes of the slice: x: 4, y: 4, z: 8, core: 2. Of those that a mesh axis runs over, the one named last changes fastest.
Arguments:
- activations: bfloat16 [32768, 2048], P(('dp', 'expert')), may hold values from -6 to 6
- routes: int32 [32768, 8], P(('dp', 'expert')), may hold values from 0 to 127, as said below
- gates: float32 [32768, 8], P(('dp', 'expert')), may hold values from 0.05 to 1
- gate_levels: bfloat16 [16, 2048, 768], P('expert'), may hold values from -8 to 7, as said below
- gate_scales: float32 [16, 16, 768], P('expert'), may hold values from 0.0022097088 to 0.008838835
- up_levels: bfloat16 [16, 2048, 768], P('expert'), may hold values from -8 to 7, as said below
- up_scales: float32 [16, 16, 768], P('expert'), may hold values from 0.0022097088 to 0.008838835
- down_levels: bfloat16 [16, 768, 2048], P('expert'), may hold values from -8 to 7, as said below
- down_scales: float32 [16, 6, 2048], P('expert'), may hold values from 0.0036084391 to 0.0144337565
- gate_adapter_first: bfloat16 [16, 16, 2048], P('expert'), may hold values from -0.125 to 0.125
- gate_adapter_second: bfloat16 [16, 16, 768], P('expert'), may hold values from -1.5 to 1.5
- up_adapter_first: bfloat16 [16, 16, 2048], P('expert'), may hold values from -0.125 to 0.125
- up_adapter_second: bfloat16 [16, 16, 768], P('expert'), may hold values from -1.5 to 1.5
- down_adapter_first: bfloat16 [16, 16, 768], P('expert'), may hold values from -0.21875 to 0.21875
- down_adapter_second: bfloat16 [16, 16, 2048], P('expert'), may hold values from -1.5 to 1.5
- upstream: bfloat16 [32768, 2048], P(('dp', 'expert')), may hold values from -6 to 6
Outputs:
- mixed: bfloat16 [32768, 2048], P(('dp', 'expert'))
- input_grad: bfloat16 [32768, 2048], P(('dp', 'expert'))
- grad_wide: float32 [16, 3, 16, 2048], P('expert', None, None, 'dp')
- grad_narrow: float32 [16, 3, 16, 768], P('expert', None, 'dp')
The draws below stay inside these ranges and needn't reach their ends.
Inputs may be any that keep to these rules, and one draw needn't show every extreme that they name: `routes`: each row names 8 different experts. No expert is named by more than 16 rows of one device, and some expert below 16 is named by exactly 16 rows of every device. `gate_levels`: whole numbers. `up_levels`: whole numbers. `down_levels`: whole numbers.
All inputs are finite; a program needn't handle non-finite values.
Results may differ from the reference program's by a relative error of at most 0.011.
Values may be sent and summed in bfloat16 or wider, within the bound.
No kernel may reach another device: no remote copies, remote signals or barrier semaphores. Data moves between devices by JAX's collectives and lax.ppermute only.
A program may use at most 128 MiB of HBM per device.

```python
import math
import jax
import jax.numpy as jnp
from jax import lax

D = 2048
FF = 768
GROUP = 128
ROUTED = 128
TOP = 8
RANK = 16
TOK_DEV = 128
CAP = 16
WINDOW = 16
TOKENS = 32768


def draw_routes(key, part):
    key = jax.random.fold_in(key, 7)
    blocks = TOKENS // TOK_DEV
    share = TOK_DEV * TOP // ROUTED
    favour_key, block_key = jax.random.split(key)
    favoured = jax.random.randint(favour_key, (), 0, WINDOW)
    position = jnp.arange(TOK_DEV * TOP, dtype=jnp.int32)
    level = jnp.where(position < 64 * share, position // (2 * share), 32 + (position - 64 * share) // share).astype(jnp.int32)

    def one_block(subkey):
        score_key, row_key, column_key = jax.random.split(subkey, 3)
        index = jnp.arange(ROUTED, dtype=jnp.int32)
        scores = jax.random.randint(score_key, (ROUTED,), 0, 1 << 20) * ROUTED + index
        scores = jnp.where(index == favoured, -1, scores)
        order = jnp.argsort(scores, stable=True).astype(jnp.int32)
        listing = order[level].reshape(TOP, TOK_DEV).T
        listing = listing[jax.random.permutation(row_key, TOK_DEV)]
        column_scores = jax.random.randint(column_key, (TOK_DEV, TOP), 0, 1 << 20) * TOP + jnp.arange(TOP, dtype=jnp.int32)[None, :]
        column_order = jnp.argsort(column_scores, axis=1, stable=True)
        return jnp.take_along_axis(listing, column_order, axis=1)
    drawn = jax.vmap(one_block)(jax.random.split(block_key, blocks))
    return drawn.reshape(TOKENS, TOP).astype(jnp.int32)


def draw_gate_levels(key, part):
    key = jax.random.fold_in(key, 11)
    return jax.random.randint(key, (WINDOW, D, FF), -8, 8).astype(jnp.bfloat16)


def draw_up_levels(key, part):
    key = jax.random.fold_in(key, 12)
    return jax.random.randint(key, (WINDOW, D, FF), -8, 8).astype(jnp.bfloat16)


def draw_down_levels(key, part):
    key = jax.random.fold_in(key, 13)
    return jax.random.randint(key, (WINDOW, FF, D), -8, 8).astype(jnp.bfloat16)


def shard_levels(own_key, extent, shards, low, top_value):
    level, own = 1.0, jax.random.fold_in(own_key, 6)
    for dim, shards_of in shards:
        draws = jnp.exp(jax.random.uniform(jax.random.fold_in(own, dim), (shards_of,), jnp.float32, low / len(shards), top_value / len(shards)))
        level = level * jnp.repeat(draws, extent[dim] // shards_of).reshape([-1 if axis == dim else 1 for axis in range(len(extent))])
    return level


def scatter_about(stream_key, shape, scale, reach, pieces=(), kind=jnp.bfloat16):
    loudness = shard_levels(stream_key, shape, pieces, -0.22, 0.18) if pieces else 1.0
    values = jax.random.normal(stream_key, shape, jnp.float32) * scale * loudness
    return jnp.minimum(jnp.maximum(values, -reach), reach).astype(kind)


def setup_inputs(seed: int = 0) -> dict:
    streams_of = jax.random.split(jax.random.key(seed), 17)
    return {
        "activations": scatter_about(streams_of[0], (TOKENS, D), 1.0, 6.0, ((0, 256),)),
        "routes": draw_routes(jax.random.fold_in(streams_of[16], 71), 0),
        "gates": jnp.clip(jnp.exp(math.log(1.0) - 2.9957323 * jax.random.uniform(streams_of[2], (TOKENS, TOP), jnp.float32) ** shard_levels(streams_of[2], (TOKENS, TOP), ((0, 256),), -0.2, 0.2)), 0.05, 1.0),
        "gate_levels": draw_gate_levels(jax.random.fold_in(streams_of[16], 71), 0),
        "gate_scales": jnp.clip(jnp.exp(math.log(0.008838835) - 1.3862944 * jax.random.uniform(streams_of[4], (WINDOW, D // GROUP, FF), jnp.float32) ** shard_levels(streams_of[4], (WINDOW, D // GROUP, FF), ((0, 16),), -0.2, 0.2)), 0.0022097088, 0.008838835),
        "up_levels": draw_up_levels(jax.random.fold_in(streams_of[16], 71), 0),
        "up_scales": jnp.clip(jnp.exp(math.log(0.008838835) - 1.3862944 * jax.random.uniform(streams_of[6], (WINDOW, D // GROUP, FF), jnp.float32) ** shard_levels(streams_of[6], (WINDOW, D // GROUP, FF), ((0, 16),), -0.2, 0.2)), 0.0022097088, 0.008838835),
        "down_levels": draw_down_levels(jax.random.fold_in(streams_of[16], 71), 0),
        "down_scales": jnp.clip(jnp.exp(math.log(0.0144337565) - 1.3862944 * jax.random.uniform(streams_of[8], (WINDOW, FF // GROUP, D), jnp.float32) ** shard_levels(streams_of[8], (WINDOW, FF // GROUP, D), ((0, 16),), -0.2, 0.2)), 0.0036084391, 0.0144337565),
        "gate_adapter_first": scatter_about(streams_of[9], (WINDOW, RANK, D), D ** -0.5, 0.125, ((0, 16),)),
        "gate_adapter_second": scatter_about(streams_of[10], (WINDOW, RANK, FF), RANK ** -0.5, 1.5, ((0, 16),)),
        "up_adapter_first": scatter_about(streams_of[11], (WINDOW, RANK, D), D ** -0.5, 0.125, ((0, 16),)),
        "up_adapter_second": scatter_about(streams_of[12], (WINDOW, RANK, FF), RANK ** -0.5, 1.5, ((0, 16),)),
        "down_adapter_first": scatter_about(streams_of[13], (WINDOW, RANK, FF), FF ** -0.5, 0.21875, ((0, 16),)),
        "down_adapter_second": scatter_about(streams_of[14], (WINDOW, RANK, D), RANK ** -0.5, 1.5, ((0, 16),)),
        "upstream": scatter_about(streams_of[15], (TOKENS, D), 1.0, 6.0, ((0, 256),)),
    }


ADAPTER_SCALING = 0.5

def matrix_product(left_operand, right_operand):
    return lax.dot_general(left_operand, right_operand, (((1,), (1,)), ((), ())), preferred_element_type=jnp.float32)

def product_result(left_operand, right_operand):
    return jnp.dot(left_operand, right_operand, preferred_element_type=jnp.float32)

def rank_grad(left_operand, right_operand):
    return ADAPTER_SCALING * lax.dot_general(left_operand, right_operand, (((0,), (0,)), ((), ())), preferred_element_type=jnp.float32)

def dequantize(levels, scales):
    return (levels.astype(jnp.float32) * jnp.repeat(scales.astype(jnp.float32), GROUP, axis=0)).astype(jnp.bfloat16)

def forward_part(input_rows, params):
    gate_base_weight, up_base_weight, down_base_weight, gate_adapter_first, gate_adapter_second, up_adapter_first, up_adapter_second, down_adapter_first, down_adapter_second = params
    gate_lowrank = matrix_product(input_rows, gate_adapter_first).astype(jnp.bfloat16)
    up_lowrank = matrix_product(input_rows, up_adapter_first).astype(jnp.bfloat16)
    gate_preactivation = product_result(input_rows, gate_base_weight) + ADAPTER_SCALING * product_result(gate_lowrank, gate_adapter_second)
    up_preactivation = product_result(input_rows, up_base_weight) + ADAPTER_SCALING * product_result(up_lowrank, up_adapter_second)
    logistic = jax.nn.sigmoid(gate_preactivation)
    activated = gate_preactivation * logistic
    hidden_state = (activated * up_preactivation).astype(jnp.bfloat16)
    down_lowrank = matrix_product(hidden_state, down_adapter_first).astype(jnp.bfloat16)
    output_rows = (product_result(hidden_state, down_base_weight) + ADAPTER_SCALING * product_result(down_lowrank, down_adapter_second)).astype(jnp.bfloat16)
    return (output_rows, (gate_lowrank, up_lowrank, gate_preactivation, up_preactivation, logistic, activated, hidden_state, down_lowrank))

def backward_down(output_gradient, stored, params):
    gate_base_weight, up_base_weight, down_base_weight, gate_adapter_first, gate_adapter_second, up_adapter_first, up_adapter_second, down_adapter_first, down_adapter_second = params
    hidden_state, down_lowrank = (stored[6], stored[7])
    down_backprop = matrix_product(output_gradient, down_adapter_second).astype(jnp.bfloat16)
    hidden_gradient = matrix_product(output_gradient, down_base_weight) + ADAPTER_SCALING * product_result(down_backprop, down_adapter_first)
    return (hidden_gradient, rank_grad(down_lowrank, output_gradient), rank_grad(down_backprop, hidden_state))

def backward_rest(input_rows, hidden_gradient, stored, params):
    gate_base_weight, up_base_weight, down_base_weight, gate_adapter_first, gate_adapter_second, up_adapter_first, up_adapter_second, down_adapter_first, down_adapter_second = params
    gate_lowrank, up_lowrank, gate_preactivation, up_preactivation, logistic, activated = stored[:6]
    d_gate = (hidden_gradient * up_preactivation * logistic * (1.0 + gate_preactivation * (1.0 - logistic))).astype(jnp.bfloat16)
    d_up = (hidden_gradient * activated).astype(jnp.bfloat16)
    gate_backprop = matrix_product(d_gate, gate_adapter_second).astype(jnp.bfloat16)
    up_backprop = matrix_product(d_up, up_adapter_second).astype(jnp.bfloat16)
    row_gradient = matrix_product(d_gate, gate_base_weight) + matrix_product(d_up, up_base_weight)
    row_gradient = (row_gradient + ADAPTER_SCALING * (product_result(gate_backprop, gate_adapter_first) + product_result(up_backprop, up_adapter_first))).astype(jnp.bfloat16)
    grads = (rank_grad(gate_backprop, input_rows), rank_grad(up_backprop, input_rows), rank_grad(gate_lowrank, d_gate), rank_grad(up_lowrank, d_up))
    return (row_gradient, grads)

def slot_tables(block_routes, block_gates):
    flat_routes = block_routes.reshape(-1).astype(jnp.int32)
    columns = jnp.arange(WINDOW, dtype=jnp.int32)
    onehot = (flat_routes[:, None] == columns[None, :]).astype(jnp.int32)
    before = (jnp.cumsum(onehot, axis=0) - onehot).astype(jnp.int32)
    place = lax.optimization_barrier(jnp.sum(before * onehot, axis=1)).astype(jnp.int32)
    slot_of = jnp.where(flat_routes < WINDOW, flat_routes * CAP + place, WINDOW * CAP).astype(jnp.int32)
    owner_row = (jnp.arange(TOK_DEV * TOP, dtype=jnp.int32) // TOP).astype(jnp.int32)
    source_of = jnp.full((WINDOW * CAP + 1,), TOK_DEV, jnp.int32).at[slot_of].set(owner_row)[:WINDOW * CAP]
    weight_of = jnp.zeros((WINDOW * CAP + 1,), jnp.float32).at[slot_of].set(block_gates.reshape(-1))[:WINDOW * CAP]
    return (source_of, weight_of)

def reference(activations, routes, gates, gate_levels, gate_scales, up_levels, up_scales, down_levels, down_scales, gate_adapter_first, gate_adapter_second, up_adapter_first, up_adapter_second, down_adapter_first, down_adapter_second, upstream):
    blocks = TOKENS // TOK_DEV
    source_of, weight_of = jax.vmap(slot_tables)(routes.reshape(blocks, TOK_DEV, TOP), gates.reshape(blocks, TOK_DEV, TOP))
    offsets = (jnp.arange(blocks, dtype=jnp.int32) * TOK_DEV)[:, None]
    global_row = jnp.where(source_of < TOK_DEV, source_of + offsets, TOKENS).astype(jnp.int32)
    global_row = global_row.reshape(blocks, WINDOW, CAP).transpose(1, 0, 2).reshape(WINDOW, blocks * CAP)
    slot_gate = weight_of.reshape(blocks, WINDOW, CAP).transpose(1, 0, 2).reshape(WINDOW, blocks * CAP)
    zero_row = jnp.zeros((1, D), activations.dtype)
    token_pad = jnp.concatenate([activations, zero_row], axis=0)
    upstream_pad = jnp.concatenate([upstream, zero_row], axis=0)

    def one_expert(carry, inputs):
        mixed_acc, input_acc = carry
        row_index, slot_weight = (inputs[0], inputs[1])
        frozen = (dequantize(inputs[2], inputs[3]), dequantize(inputs[4], inputs[5]), dequantize(inputs[6], inputs[7]))
        params = frozen + tuple(inputs[8:])
        input_rows = token_pad[row_index]
        output_gradient = (slot_weight[:, None] * upstream_pad[row_index].astype(jnp.float32)).astype(jnp.bfloat16)
        output_rows, stored = forward_part(input_rows, params)
        hidden_gradient, grad_down_outer, grad_down_inner = backward_down(output_gradient, stored, params)
        row_gradient, grads = backward_rest(input_rows, hidden_gradient, stored, params)
        mixed_acc = mixed_acc.at[row_index].add(slot_weight[:, None] * output_rows.astype(jnp.float32))
        input_acc = input_acc.at[row_index].add(row_gradient.astype(jnp.float32))
        wide = jnp.stack([grads[0], grads[1], grad_down_outer])
        narrow = jnp.stack([grads[2], grads[3], grad_down_inner])
        return ((mixed_acc, input_acc), (wide, narrow))
    start = jnp.zeros((TOKENS + 1, D), jnp.float32)
    carried, stacked = lax.scan(one_expert, (start, start), (global_row, slot_gate, gate_levels, gate_scales, up_levels, up_scales, down_levels, down_scales, gate_adapter_first, gate_adapter_second, up_adapter_first, up_adapter_second, down_adapter_first, down_adapter_second))
    mixed = carried[0][:TOKENS].astype(jnp.bfloat16)
    input_grad = carried[1][:TOKENS].astype(jnp.bfloat16)
    return (mixed, input_grad, stacked[0], stacked[1])
```

```python
import jax
import jax.numpy as jnp
from jax import lax
from jax.experimental import pallas as pl
from jax.experimental.pallas import tpu as pltpu
from jax.sharding import PartitionSpec as P

GROUP = 128
CAP = 16
SCALING = 0.5
BF = jnp.bfloat16
F32 = jnp.float32
VMEM = pl.BlockSpec(memory_space=pltpu.VMEM)
SMEM = pl.BlockSpec(memory_space=pltpu.SMEM)
LIMIT = 48 * 1024 * 1024


def nn(a, b):
    return lax.dot_general(a, b, (((1,), (0,)), ((), ())), preferred_element_type=F32)


def nt(a, b):
    return lax.dot_general(a, b, (((1,), (1,)), ((), ())), preferred_element_type=F32)


def tn(a, b):
    return lax.dot_general(a, b, (((0,), (0,)), ((), ())), preferred_element_type=F32)


def params(cost=None):
    return pltpu.CompilerParams(vmem_limit_bytes=LIMIT)


def cost(flops, bytes_accessed):
    return pl.CostEstimate(flops=flops, bytes_accessed=bytes_accessed, transcendentals=0)


def slot_tables(routes, gates, experts):
    tokens, top = routes.shape
    routes_t = routes.astype(F32).T
    gates_t = gates.T
    column = lax.broadcasted_iota(jnp.int32, (experts, tokens), 0).astype(F32)
    named = jnp.zeros((experts, tokens), F32)
    weight = jnp.zeros((experts, tokens), F32)
    for k in range(top):
        hit = routes_t[k : k + 1, :] == column
        named = named + jnp.where(hit, 1.0, 0.0)
        weight = weight + jnp.where(hit, gates_t[k : k + 1, :], 0.0)
    earlier = lax.broadcasted_iota(jnp.int32, (tokens, tokens), 0)
    later = lax.broadcasted_iota(jnp.int32, (tokens, tokens), 1)
    before = jnp.where(earlier < later, 1.0, 0.0).astype(BF)
    place = nn(named.astype(BF), before)
    place = jnp.where(named > 0.0, place, -1.0)
    slot = lax.broadcasted_iota(jnp.int32, (experts, CAP, tokens), 1).astype(F32)
    taken = place[:, None, :] == slot
    one = jnp.where(taken, 1.0, 0.0).reshape(experts * CAP, tokens)
    gate = jnp.where(taken, weight[:, None, :], 0.0).reshape(experts * CAP, tokens)
    return one, gate


def dispatch_kernel(routes_ref, gates_ref, act_ref, up_ref, send_ref):
    experts = send_ref.shape[0]
    width = act_ref.shape[1]
    one, gate = slot_tables(routes_ref[...], gates_ref[...], experts)
    one = one.astype(BF)
    weight = jnp.sum(gate, axis=1, keepdims=True)
    step = 512
    for lo in range(0, width, step):
        cols = slice(lo, lo + step)
        send_ref[:, :CAP, cols] = nn(one, act_ref[:, cols]).astype(BF).reshape(experts, CAP, step)
        picked = weight * nn(one, up_ref[:, cols])
        send_ref[:, CAP:, cols] = picked.astype(BF).reshape(experts, CAP, step)


def dispatch(routes, gates, activations, upstream, experts):
    width = activations.shape[1]
    return pl.pallas_call(
        dispatch_kernel,
        out_shape=jax.ShapeDtypeStruct((experts, 2 * CAP, width), BF),
        in_specs=[VMEM] * 4,
        out_specs=VMEM,
        compiler_params=params(),
        name="dispatch",
    )(routes, gates, activations, upstream)


def tables_kernel(routes_ref, gates_ref, one_ref, high_ref, low_ref):
    experts = one_ref.shape[0] // CAP
    one, gate = slot_tables(routes_ref[...], gates_ref[...], experts)
    high = gate.astype(BF)
    one_ref[...] = one.astype(BF)
    high_ref[...] = high
    low_ref[...] = (gate - high.astype(F32)).astype(BF)


def tables(routes, gates, experts):
    shape = jax.ShapeDtypeStruct((experts * CAP, routes.shape[0]), BF)
    return pl.pallas_call(
        tables_kernel,
        out_shape=(shape, shape, shape),
        in_specs=[VMEM] * 2,
        out_specs=(VMEM,) * 3,
        compiler_params=params(),
        name="tables",
    )(routes, gates)


def combine_kernel(got_ref, one_ref, high_ref, low_ref, mixed_ref, grad_ref):
    experts = got_ref.shape[0]
    width = got_ref.shape[2]
    one = one_ref[...]
    high = high_ref[...]
    low = low_ref[...]
    step = 512
    for lo in range(0, width, step):
        cols = slice(lo, lo + step)
        out = got_ref[:, :CAP, cols].reshape(experts * CAP, step)
        back = got_ref[:, CAP:, cols].reshape(experts * CAP, step)
        mixed_ref[:, cols] = (tn(high, out) + tn(low, out)).astype(BF)
        grad_ref[:, cols] = tn(one, back).astype(BF)


def combine(got, one, high, low):
    shape = jax.ShapeDtypeStruct((one.shape[1], got.shape[2]), BF)
    return pl.pallas_call(
        combine_kernel,
        out_shape=(shape, shape),
        in_specs=[VMEM] * 4,
        out_specs=(VMEM,) * 2,
        compiler_params=params(),
        name="combine",
    )(got, one, high, low)


def dequantize_kernel(levels_ref, scales_ref, frozen_ref):
    group = pl.program_id(0)
    per_step = levels_ref.shape[0] // GROUP
    for i in range(per_step):
        rows = slice(i * GROUP, (i + 1) * GROUP)
        scale = scales_ref[pl.ds(group * per_step + i, 1), :]
        frozen_ref[rows, :] = (levels_ref[rows, :].astype(F32) * scale).astype(BF)


def dequantize(levels, scales, per_step):
    rows, columns = levels.shape
    block = pl.BlockSpec((per_step * GROUP, columns), lambda i: (i, 0))
    return pl.pallas_call(
        dequantize_kernel,
        grid=(rows // (per_step * GROUP),),
        out_shape=jax.ShapeDtypeStruct(levels.shape, BF),
        in_specs=[block, pl.BlockSpec(scales.shape, lambda i: (0, 0))],
        out_specs=block,
        compiler_params=params(),
        cost_estimate=cost(levels.size, levels.size * 4),
        name="dequantize",
    )(levels, scales)


def expert_kernel(
    got_ref, gate_ref, up_ref, down_ref, first_ref, gate_second_ref, up_second_ref, down_first_ref,
    down_second_ref, send_ref, hidden_ref, d_gate_ref, d_up_ref, low_ref,
):
    experts, _, width = got_ref.shape
    rows = experts * CAP
    inner = gate_ref.shape[1]
    step = 256
    x = got_ref[:, :CAP, :].reshape(rows, width)
    g = got_ref[:, CAP:, :].reshape(rows, width)
    first_low = nt(x, first_ref[...]).astype(BF)
    rank = first_low.shape[1] // 2
    gate_low, up_low = first_low[:, :rank], first_low[:, rank:]
    back_down = nt(g, down_second_ref[...]).astype(BF)
    half = jnp.asarray(SCALING, BF)
    down_low = jnp.zeros((rows, rank), F32)
    back_gate = jnp.zeros((rows, rank), F32)
    back_up = jnp.zeros((rows, rank), F32)
    for lo in range(0, inner, step):
        cols = slice(lo, lo + step)
        gate_pre = nn(x, gate_ref[:, cols]) + nn(gate_low * half, gate_second_ref[:, cols])
        up_pre = nn(x, up_ref[:, cols]) + nn(up_low * half, up_second_ref[:, cols])
        d_hidden = nt(g, down_ref[cols, :]) + nn(back_down * half, down_first_ref[:, cols])
        logistic = jax.nn.sigmoid(gate_pre)
        activated = gate_pre * logistic
        hidden = (activated * up_pre).astype(BF)
        d_gate = (d_hidden * up_pre * logistic * (1.0 + gate_pre * (1.0 - logistic))).astype(BF)
        d_up = (d_hidden * activated).astype(BF)
        hidden_ref[:, cols] = hidden
        d_gate_ref[:, cols] = d_gate
        d_up_ref[:, cols] = d_up
        down_low += nt(hidden, down_first_ref[:, cols])
        back_gate += nt(d_gate, gate_second_ref[:, cols])
        back_up += nt(d_up, up_second_ref[:, cols])
    down_low = down_low.astype(BF)
    back_both = jnp.concatenate([back_gate, back_up], axis=1).astype(BF)
    low_ref[...] = jnp.concatenate([first_low, back_down, down_low, back_both], axis=1)
    hidden = hidden_ref[...]
    d_gate = d_gate_ref[...]
    d_up = d_up_ref[...]
    for lo in range(0, width, step):
        cols = slice(lo, lo + step)
        out = nn(hidden, down_ref[:, cols]) + nn(down_low * half, down_second_ref[:, cols])
        send_ref[:, :CAP, cols] = out.astype(BF).reshape(experts, CAP, step)
        back = nt(d_gate, gate_ref[cols, :]) + nt(d_up, up_ref[cols, :])
        back = back + nn(back_both * half, first_ref[:, cols])
        send_ref[:, CAP:, cols] = back.astype(BF).reshape(experts, CAP, step)


def expert(got, gate, up, down, first, gate_second, up_second, down_first, down_second):
    rows = got.shape[0] * CAP
    inner = gate.shape[1]
    wide = jax.ShapeDtypeStruct((rows, inner), BF)
    return pl.pallas_call(
        expert_kernel,
        out_shape=(
            jax.ShapeDtypeStruct(got.shape, BF), wide, wide, wide,
            jax.ShapeDtypeStruct((rows, 6 * gate_second.shape[0]), BF),
        ),
        in_specs=[VMEM] * 9,
        out_specs=(VMEM,) * 5,
        compiler_params=params(),
        name="expert",
    )(got, gate, up, down, first, gate_second, up_second, down_first, down_second)


def grads_kernel(group_ref, got_ref, hidden_ref, d_gate_ref, d_up_ref, low_ref, keep_ref, send_ref, piece_ref):
    experts, _, width = got_ref.shape
    rows = experts * CAP
    groups = piece_ref.shape[0]
    inner = hidden_ref.shape[1]
    rank = low_ref.shape[1] // 6
    low = low_ref[...]
    gate_low, up_low, back_down, down_low = (low[:, i * rank : (i + 1) * rank] for i in range(4))
    back_both = low[:, 4 * rank :]
    column = width // groups
    step = 512
    for lo in range(0, width, step):
        cols = slice(lo, lo + step)
        x = got_ref[:, :CAP, cols].reshape(rows, step)
        g = got_ref[:, CAP:, cols].reshape(rows, step)
        both = SCALING * tn(back_both, x)
        down = SCALING * tn(down_low, g)
        for i in range(step // column):
            piece = lo // column + i
            part = slice(i * column, (i + 1) * column)
            piece_ref[piece, : 2 * rank, :] = both[:, part]
            piece_ref[piece, 2 * rank : 3 * rank, :] = down[:, part]
    source = lax.broadcasted_iota(jnp.int32, (rank, 8 * rank), 0)
    target = lax.broadcasted_iota(jnp.int32, (rank, 8 * rank), 1)
    narrow = jnp.zeros((8 * rank, inner), F32)
    for i, (left, right) in enumerate(((gate_low, d_gate_ref), (up_low, d_up_ref), (back_down, hidden_ref))):
        spread = jnp.where(target == 8 * source + i, 1.0, 0.0).astype(BF)
        narrow += tn(nn(left, spread).astype(BF), right[...])
    narrow = SCALING * narrow
    for piece in range(groups):
        for i in range(inner // column):
            at = 3 * rank + 8 * i
            piece_ref[piece, at : at + 8, :] = narrow[8 * piece : 8 * piece + 8, i * column : (i + 1) * column]
    group = group_ref[0]
    side = group % 2
    plane = group // 2
    for place in range(groups // 2):
        turned = (place & 1) * 4 + (place & 2) + (place >> 2)
        other = lax.bitwise_xor(plane, jnp.int32(turned))
        keep_ref[place] = piece_ref[2 * other + side]
        send_ref[place] = piece_ref[2 * other + 1 - side]


def adapter_grads(group, got, hidden, d_gate, d_up, low, groups):
    width = got.shape[2]
    inner = hidden.shape[1]
    rank = low.shape[1] // 6
    column = width // groups
    height = 3 * rank + 8 * (inner // column)
    shape = jax.ShapeDtypeStruct((groups // 2, height, column), F32)
    return pl.pallas_call(
        grads_kernel,
        out_shape=(shape, shape),
        in_specs=[SMEM] + [VMEM] * 5,
        out_specs=(VMEM,) * 2,
        scratch_shapes=[pltpu.VMEM((groups, height, column), F32)],
        compiler_params=params(),
        name="adapter_grads",
    )(group, got, hidden, d_gate, d_up, low)


def shards(
    activations, routes, gates, gate_levels, gate_scales, up_levels, up_scales, down_levels, down_scales,
    gate_adapter_first, gate_adapter_second, up_adapter_first, up_adapter_second,
    down_adapter_first, down_adapter_second, upstream,
):
    experts = lax.axis_size("expert")
    groups = lax.axis_size("dp")
    width = activations.shape[1]
    inner = gate_levels.shape[2]
    rank = gate_adapter_first.shape[1]

    send = dispatch(routes, gates, activations, upstream, experts)
    got = lax.all_to_all(send, "expert", split_axis=0, concat_axis=0, tiled=True)

    gate = dequantize(gate_levels[0], gate_scales[0], 4)
    up = dequantize(up_levels[0], up_scales[0], 4)
    down = dequantize(down_levels[0], down_scales[0], 2)
    first = jnp.concatenate([gate_adapter_first[0], up_adapter_first[0]], axis=0)
    one, high, low_part = tables(routes, gates, experts)

    send, hidden, d_gate, d_up, low = expert(
        got, gate, up, down, first, gate_adapter_second[0], up_adapter_second[0],
        down_adapter_first[0], down_adapter_second[0],
    )
    back = lax.all_to_all(send, "expert", split_axis=0, concat_axis=0, tiled=True)

    group = lax.axis_index("dp").astype(jnp.int32).reshape(1)
    keep, other = adapter_grads(group, got, hidden, d_gate, d_up, low, groups)
    total = keep + lax.ppermute(other, "dp", [(i, i ^ 1) for i in range(groups)])
    mask = 2
    while total.shape[0] > 1:
        half = total.shape[0] // 2
        total = total[:half] + lax.ppermute(total[half:], "dp", [(i, i ^ mask) for i in range(groups)])
        mask *= 2
    column = width // groups
    grad_wide = total[0, : 3 * rank].reshape(1, 3, rank, column)
    narrow = total[0, 3 * rank :].reshape(inner // column, 8, column)[:, :3]
    grad_narrow = narrow.transpose(1, 0, 2).reshape(1, 3, 1, inner)

    mixed, input_grad = combine(back, one, high, low_part)
    return mixed, input_grad, grad_wide, grad_narrow


def solution(mesh):
    rows = P(("dp", "expert"), None)
    weight = P("expert", None, None)
    return jax.shard_map(
        shards,
        mesh=mesh,
        in_specs=(rows,) * 3 + (weight,) * 12 + (rows,),
        out_specs=(rows, rows, P("expert", None, None, "dp"), P("expert", None, "dp", None)),
        check_vma=False,
    )
```

```python
import jax
import jax.numpy as jnp
from jax import lax
from jax.experimental import pallas as pl
from jax.experimental.pallas import tpu as pltpu
from jax.sharding import PartitionSpec as P

GROUP = 128
CAP = 16
SCALING = 0.5
BF = jnp.bfloat16
F32 = jnp.float32
VMEM = pl.BlockSpec(memory_space=pltpu.VMEM)
SMEM = pl.BlockSpec(memory_space=pltpu.SMEM)
HBM = pl.BlockSpec(memory_space=pltpu.HBM)
DMA = pltpu.SemaphoreType.DMA
SPLITS = {1280: 1280, 2048: 768}


def nn(a, b):
    return lax.dot_general(a, b, (((1,), (0,)), ((), ())), preferred_element_type=F32)


def nt(a, b):
    return lax.dot_general(a, b, (((1,), (1,)), ((), ())), preferred_element_type=F32)


def tn(a, b):
    return lax.dot_general(a, b, (((0,), (0,)), ((), ())), preferred_element_type=F32)


def params(mebibytes):
    return pltpu.CompilerParams(vmem_limit_bytes=mebibytes * 1024 * 1024)


def cost(flops, bytes_accessed):
    return pl.CostEstimate(flops=flops, bytes_accessed=bytes_accessed, transcendentals=0)


def in_vmem(array):
    return pltpu.with_memory_space_constraint(array, pltpu.VMEM)


def in_hbm(array):
    return pltpu.with_memory_space_constraint(array, pltpu.HBM)


def slot_tables(routes, gates_t, experts):
    top, tokens = routes.shape
    routes_t = routes.astype(F32)
    column = lax.broadcasted_iota(jnp.int32, (experts, tokens), 0).astype(F32)
    named = jnp.zeros((experts, tokens), F32)
    weight = jnp.zeros((experts, tokens), F32)
    for k in range(top):
        hit = routes_t[k : k + 1, :] == column
        named = named + jnp.where(hit, 1.0, 0.0)
        weight = weight + jnp.where(hit, gates_t[k : k + 1, :], 0.0)
    earlier = lax.broadcasted_iota(jnp.int32, (tokens, tokens), 0)
    later = lax.broadcasted_iota(jnp.int32, (tokens, tokens), 1)
    before = jnp.where(earlier < later, 1.0, 0.0).astype(BF)
    place = nn(named.astype(BF), before)
    place = jnp.where(named > 0.0, place, -1.0)
    slot = lax.broadcasted_iota(jnp.int32, (experts, CAP, tokens), 1).astype(F32)
    taken = place[:, None, :] == slot
    one = jnp.where(taken, 1.0, 0.0).reshape(experts * CAP, tokens)
    gate = jnp.where(taken, weight[:, None, :], 0.0).reshape(experts * CAP, tokens)
    return one, gate


def dispatch_kernel(
    routes_hbm, gates_hbm, act_hbm, up_hbm, send_hbm, routes_ref, gates_ref, act_ref, up_ref, send_ref, in_sem, out_sem
):
    experts = send_ref.shape[0]
    width = act_ref.shape[1]
    pairs = ((routes_hbm, routes_ref), (gates_hbm, gates_ref), (act_hbm, act_ref), (up_hbm, up_ref))
    loads = [pltpu.make_async_copy(source, target, in_sem.at[i]) for i, (source, target) in enumerate(pairs)]
    for load in loads:
        load.start()
    loads[0].wait()
    loads[1].wait()
    one, gate = slot_tables(routes_ref[...], gates_ref[...], experts)
    one = one.astype(BF)
    weight = jnp.sum(gate, axis=1, keepdims=True)
    loads[2].wait()
    loads[3].wait()
    step = 512
    stores = []
    for i, lo in enumerate(range(0, width, step)):
        cols = slice(lo, lo + step)
        send_ref[:, :CAP, cols] = nn(one, act_ref[:, cols]).astype(BF).reshape(experts, CAP, step)
        picked = weight * nn(one, up_ref[:, cols])
        send_ref[:, CAP:, cols] = picked.astype(BF).reshape(experts, CAP, step)
        store = pltpu.make_async_copy(send_ref.at[:, :, cols], send_hbm.at[:, :, cols], out_sem.at[i])
        store.start()
        stores.append(store)
    for store in stores:
        store.wait()


def dispatch(routes, gates, activations, upstream, experts):
    width = activations.shape[1]
    shape = (experts, 2 * CAP, width)
    return pl.pallas_call(
        dispatch_kernel,
        out_shape=pltpu.HBM(shape, BF),
        in_specs=[HBM] * 4,
        out_specs=HBM,
        scratch_shapes=[
            pltpu.VMEM(routes.shape, jnp.int32), pltpu.VMEM(gates.shape, F32), pltpu.VMEM(activations.shape, BF),
            pltpu.VMEM(upstream.shape, BF), pltpu.VMEM(shape, BF), DMA((4,)), DMA((4,)),
        ],
        compiler_params=params(12),
        name="dispatch",
    )(*(in_hbm(array) for array in (routes, gates, activations, upstream)))


def tables_kernel(routes_ref, gates_ref, table_ref):
    slots = table_ref.shape[2]
    one, gate = slot_tables(routes_ref[...], gates_ref[...], slots // CAP)
    one, gate = one.T, gate.T
    high = gate.astype(BF)
    table_ref[0] = one.astype(BF)
    table_ref[1] = high
    table_ref[2] = (gate - high.astype(F32)).astype(BF)


def tables(routes, gates, experts):
    return pl.pallas_call(
        tables_kernel,
        out_shape=jax.ShapeDtypeStruct((3, routes.shape[1], experts * CAP), BF),
        in_specs=[VMEM] * 2,
        out_specs=VMEM,
        compiler_params=params(4),
        name="tables",
    )(routes, gates)


def combine_kernel(got_ref, table_hbm, mixed_hbm, grad_hbm, table_ref, mixed_ref, grad_ref, in_sem, out_sem):
    load = pltpu.make_async_copy(table_hbm, table_ref, in_sem)
    load.start()
    experts = got_ref.shape[0]
    width = got_ref.shape[2]
    load.wait()
    one, high, low = table_ref[0], table_ref[1], table_ref[2]
    step = 512
    stores = []
    for i, lo in enumerate(range(0, width, step)):
        cols = slice(lo, lo + step)
        out = got_ref[:, :CAP, cols].reshape(experts * CAP, step)
        back = got_ref[:, CAP:, cols].reshape(experts * CAP, step)
        mixed_ref[:, cols] = (nn(high, out) + nn(low, out)).astype(BF)
        stores.append(pltpu.make_async_copy(mixed_ref.at[:, cols], mixed_hbm.at[:, cols], out_sem.at[0, i]))
        stores[-1].start()
        grad_ref[:, cols] = nn(one, back).astype(BF)
        stores.append(pltpu.make_async_copy(grad_ref.at[:, cols], grad_hbm.at[:, cols], out_sem.at[1, i]))
        stores[-1].start()
    for store in stores:
        store.wait()


def combine(got, table):
    shape = (table.shape[1], got.shape[2])
    return pl.pallas_call(
        combine_kernel,
        out_shape=(pltpu.HBM(shape, BF),) * 2,
        in_specs=[VMEM, HBM],
        out_specs=(HBM,) * 2,
        scratch_shapes=[pltpu.VMEM(table.shape, BF), pltpu.VMEM(shape, BF), pltpu.VMEM(shape, BF), DMA, DMA((2, 4))],
        compiler_params=params(8),
        name="combine",
    )(in_vmem(got), in_hbm(table))


def expert_kernel(
    group_ref, got_ref, gate_hbm, up_hbm, down_hbm, gate_scale_hbm, up_scale_hbm, down_scale_hbm, gate_first_hbm, up_first_hbm,
    down_second_hbm, gate_second_hbm, up_second_hbm, down_first_hbm, send_hbm, keep_hbm, other_hbm,
    gate_ref, up_ref, down_ref, gate_scale_ref, up_scale_ref, down_scale_ref, wide_ref, narrow_ref, send_ref,
    inside_ref, piece_ref, level_sem, small_sem, out_sem, piece_sem,
):
    experts, _, width = got_ref.shape
    rows = experts * CAP
    inner = gate_ref.shape[1]
    rank = gate_first_hbm.shape[0]
    step = 256

    pairs = [(source, wide_ref.at[i * rank : (i + 1) * rank, :])
             for i, source in enumerate((gate_first_hbm, up_first_hbm, down_second_hbm))]
    pairs += [(source, narrow_ref.at[i * rank : (i + 1) * rank, :])
              for i, source in enumerate((gate_second_hbm, up_second_hbm, down_first_hbm))]
    pairs += [(gate_scale_hbm, gate_scale_ref), (up_scale_hbm, up_scale_ref), (down_scale_hbm, down_scale_ref)]
    small = [pltpu.make_async_copy(source, target, small_sem.at[i]) for i, (source, target) in enumerate(pairs)]
    for copy in small:
        copy.start()
    weights = ((gate_hbm, gate_ref), (up_hbm, up_ref), (down_hbm, down_ref))
    pieces = [(part, kind) for part in range(inner // step) for kind in range(3)]
    levels = []
    for part, kind in pieces:
        cols = slice(part * step, (part + 1) * step)
        place = (cols, slice(0, width)) if kind == 2 else (slice(0, width), cols)
        source, target = weights[kind]
        levels.append(pltpu.make_async_copy(source.at[place], target.at[place], level_sem.at[part, kind]))
    for copy in levels[:3]:
        copy.start()
    def land(index):
        part, kind = pieces[index]
        if kind == 2:
            for i in range(part * step // GROUP, (part + 1) * step // GROUP):
                group = slice(i * GROUP, (i + 1) * GROUP)
                down_ref[group, :] = (down_ref[group, :].astype(F32) * down_scale_ref[i]).astype(BF)
        else:
            cols = slice(part * step, (part + 1) * step)
            target, scale_ref = ((gate_ref, gate_scale_ref), (up_ref, up_scale_ref))[kind]
            for i in range(width // GROUP):
                group = slice(i * GROUP, (i + 1) * GROUP)
                target[group, cols] = (target[group, cols].astype(F32) * scale_ref[i : i + 1, cols]).astype(BF)

    x = got_ref[:, :CAP, :].reshape(rows, width)
    g = got_ref[:, CAP:, :].reshape(rows, width)
    first_ref = wide_ref.at[: 2 * rank, :]
    down_second_ref = wide_ref.at[2 * rank :, :]
    gate_second_ref = narrow_ref.at[:rank, :]
    up_second_ref = narrow_ref.at[rank : 2 * rank, :]
    down_first_ref = narrow_ref.at[2 * rank :, :]
    for copy in small:
        copy.wait()
    for copy in levels[3:]:
        copy.start()
    first_low = nt(x, first_ref[...]).astype(BF)
    gate_low, up_low = first_low[:, :rank], first_low[:, rank:]
    back_down = nt(g, down_second_ref[...]).astype(BF)
    half = jnp.asarray(SCALING, BF)
    down_low = jnp.zeros((rows, rank), F32)
    back_gate = jnp.zeros((rows, rank), F32)
    back_up = jnp.zeros((rows, rank), F32)
    for index, (part, kind) in enumerate(pieces):
        if kind == 0:
            for copy in levels[index : index + 3]:
                copy.wait()
        land(index)
        cols = slice(part * step, (part + 1) * step)
        if kind == 0:
            gate_pre = nn(x, gate_ref[:, cols]) + nn(gate_low * half, gate_second_ref[:, cols])
            logistic = jax.nn.sigmoid(gate_pre)
            activated = gate_pre * logistic
            slope = logistic * (1.0 + gate_pre * (1.0 - logistic))
        elif kind == 1:
            up_pre = nn(x, up_ref[:, cols]) + nn(up_low * half, up_second_ref[:, cols])
            hidden = (activated * up_pre).astype(BF)
            inside_ref[0, :, cols] = hidden
            down_low += nt(hidden, down_first_ref[:, cols])
        else:
            d_hidden = nt(g, down_ref[cols, :]) + nn(back_down * half, down_first_ref[:, cols])
            d_gate = (d_hidden * up_pre * slope).astype(BF)
            d_up = (d_hidden * activated).astype(BF)
            inside_ref[1, :, cols] = d_gate
            inside_ref[2, :, cols] = d_up
            back_gate += nt(d_gate, gate_second_ref[:, cols])
            back_up += nt(d_up, up_second_ref[:, cols])
    down_low = down_low.astype(BF)
    back_both = jnp.concatenate([back_gate, back_up], axis=1).astype(BF)
    hidden, d_gate, d_up = inside_ref[0], inside_ref[1], inside_ref[2]
    stores = []
    for i, lo in enumerate(range(0, width, step)):
        cols = slice(lo, lo + step)
        out = nn(hidden, down_ref[:, cols]) + nn(down_low * half, down_second_ref[:, cols])
        send_ref[:, :CAP, cols] = out.astype(BF).reshape(experts, CAP, step)
        back = nt(d_gate, gate_ref[cols, :]) + nt(d_up, up_ref[cols, :])
        back = back + nn(back_both * half, first_ref[:, cols])
        send_ref[:, CAP:, cols] = back.astype(BF).reshape(experts, CAP, step)
        if lo + step in SPLITS:
            cols = slice(lo + step - SPLITS[lo + step], lo + step)
            stores.append(pltpu.make_async_copy(send_ref.at[:, :, cols], send_hbm.at[:, :, cols], out_sem.at[i]))
            stores[-1].start()
    groups = piece_ref.shape[0]
    column = width // groups
    for lo in range(0, width, 512):
        cols = slice(lo, lo + 512)
        both = SCALING * tn(back_both, got_ref[:, :CAP, cols].reshape(rows, 512))
        down = SCALING * tn(down_low, got_ref[:, CAP:, cols].reshape(rows, 512))
        for i in range(512 // column):
            part = slice(i * column, (i + 1) * column)
            piece_ref[lo // column + i, : 2 * rank, :] = both[:, part]
            piece_ref[lo // column + i, 2 * rank : 3 * rank, :] = down[:, part]
    source = lax.broadcasted_iota(jnp.int32, (rank, 8 * rank), 0)
    target = lax.broadcasted_iota(jnp.int32, (rank, 8 * rank), 1)
    narrow = jnp.zeros((8 * rank, inner), F32)
    for i, (left, right) in enumerate(((gate_low, d_gate), (up_low, d_up), (back_down, hidden))):
        spread = jnp.where(target == 8 * source + i, SCALING, 0.0).astype(BF)
        narrow += tn(nn(left, spread).astype(BF), right)
    for piece in range(groups):
        for i in range(inner // column):
            at = 3 * rank + 8 * i
            piece_ref[piece, at : at + 8, :] = narrow[8 * piece : 8 * piece + 8, i * column : (i + 1) * column]
    group = group_ref[0]
    side = group % 2
    plane = group // 2
    for place in range(groups // 2):
        turned = (place & 1) * 4 + (place & 2) + (place >> 2)
        other = lax.bitwise_xor(plane, jnp.int32(turned))
        for mine, out in ((side, keep_hbm), (1 - side, other_hbm)):
            stores.append(pltpu.make_async_copy(piece_ref.at[2 * other + mine], out.at[place], piece_sem.at[place, 0 if out is keep_hbm else 1]))
            stores[-1].start()
    for store in stores:
        store.wait()


def expert(group, groups, got, levels, scales, wide, narrow):
    rows = got.shape[0] * CAP
    width = got.shape[2]
    inner = levels[0].shape[1]
    rank = wide[0].shape[0]
    column = width // groups
    height = 3 * rank + 8 * (inner // column)
    part = (groups // 2, height, column)
    return pl.pallas_call(
        expert_kernel,
        out_shape=(pltpu.HBM(got.shape, BF), pltpu.HBM(part, F32), pltpu.HBM(part, F32)),
        in_specs=[SMEM, VMEM] + [HBM] * 12,
        out_specs=(HBM,) * 3,
        scratch_shapes=[
            *(pltpu.VMEM(level.shape, BF) for level in levels),
            *(pltpu.VMEM(scale.shape, F32) for scale in scales),
            pltpu.VMEM((3 * rank, width), BF), pltpu.VMEM((3 * rank, inner), BF),
            pltpu.VMEM(got.shape, BF), pltpu.VMEM((3, rows, inner), BF), pltpu.VMEM((groups, height, column), F32),
            DMA((inner // 256, 3)), DMA((9,)), DMA((width // 256,)), DMA((groups // 2, 2)),
        ],
        compiler_params=params(32),
        name="expert",
    )(group, in_vmem(got), *(in_hbm(array) for array in (*levels, *scales, *wide, *narrow)))


def shards(
    activations, routes, gates, gate_levels, gate_scales, up_levels, up_scales, down_levels, down_scales,
    gate_adapter_first, gate_adapter_second, up_adapter_first, up_adapter_second,
    down_adapter_first, down_adapter_second, upstream,
):
    experts = lax.axis_size("expert")
    groups = lax.axis_size("dp")
    width = activations.shape[1]
    inner = gate_levels.shape[2]
    rank = gate_adapter_first.shape[1]

    routes, gates = routes.T, gates.T
    group = lax.axis_index("dp").astype(jnp.int32).reshape(1)
    send, group = lax.optimization_barrier((dispatch(routes, gates, activations, upstream, experts), group))
    got = lax.all_to_all(send, "expert", split_axis=0, concat_axis=0, tiled=True)

    send, keep, other = expert(
        group,
        groups,
        got,
        (gate_levels[0], up_levels[0], down_levels[0]),
        (gate_scales[0], up_scales[0], down_scales.transpose(1, 0, 2)),
        (gate_adapter_first[0], up_adapter_first[0], down_adapter_second[0]),
        (gate_adapter_second[0], up_adapter_second[0], down_adapter_first[0]),
    )
    routes, gates, keep = lax.optimization_barrier((routes, gates, keep))
    table = tables(routes, gates, experts)
    back = lax.all_to_all(send, "expert", split_axis=0, concat_axis=0, tiled=True)

    def swap(part, mask):
        return lax.ppermute(part, "dp", [(i, i ^ mask) for i in range(groups)])

    total = keep + swap(other, 1)
    half = groups // 4
    total = total[:half] + swap(total[half:], 2)
    total = total[0] + (swap(total[1], 8) + swap(total[2], 4) + swap(total[3], 12))
    column = width // groups
    grad_wide = total[: 3 * rank].reshape(1, 3, rank, column)
    narrow = total[3 * rank :].reshape(inner // column, 8, column)[:, :3]
    grad_narrow = narrow.transpose(1, 0, 2).reshape(1, 3, 1, inner)

    mixed, input_grad = combine(back, table)
    return mixed, input_grad, grad_wide, grad_narrow


def solution(mesh):
    rows = P(("dp", "expert"), None)
    weight = P("expert", None, None)
    return jax.shard_map(
        shards,
        mesh=mesh,
        in_specs=(rows,) * 3 + (weight,) * 12 + (rows,),
        out_specs=(rows, rows, P("expert", None, None, "dp"), P("expert", None, "dp", None)),
        check_vma=False,
    )
```

```python
import jax
import jax.numpy as jnp
from jax import lax
from jax.experimental import pallas as pl
from jax.experimental.pallas import tpu as pltpu
from jax.sharding import PartitionSpec as P

GROUP = 128
FIRST_TO_FREEZE = 0
CAP = 16
SCALING = 0.5
BF = jnp.bfloat16
F32 = jnp.float32
VMEM = pl.BlockSpec(memory_space=pltpu.VMEM)
SMEM = pl.BlockSpec(memory_space=pltpu.SMEM)
HBM = pl.BlockSpec(memory_space=pltpu.HBM)
DMA = pltpu.SemaphoreType.DMA
SPLITS = {1280: 1280, 2048: 768}


def nn(a, b):
    return lax.dot_general(a, b, (((1,), (0,)), ((), ())), preferred_element_type=F32)


def nt(a, b):
    return lax.dot_general(a, b, (((1,), (1,)), ((), ())), preferred_element_type=F32)


def tn(a, b):
    return lax.dot_general(a, b, (((0,), (0,)), ((), ())), preferred_element_type=F32)


def params(mebibytes):
    return pltpu.CompilerParams(vmem_limit_bytes=mebibytes * 1024 * 1024)


def cost(flops, bytes_accessed):
    return pl.CostEstimate(flops=flops, bytes_accessed=bytes_accessed, transcendentals=0)


def in_vmem(array):
    return pltpu.with_memory_space_constraint(array, pltpu.VMEM)


def in_hbm(array):
    return pltpu.with_memory_space_constraint(array, pltpu.HBM)


def slot_tables(routes, gates_t, experts):
    top, tokens = routes.shape
    routes_t = routes.astype(F32)
    column = lax.broadcasted_iota(jnp.int32, (experts, tokens), 0).astype(F32)
    named = jnp.zeros((experts, tokens), F32)
    weight = jnp.zeros((experts, tokens), F32)
    for k in range(top):
        hit = routes_t[k : k + 1, :] == column
        named = named + jnp.where(hit, 1.0, 0.0)
        weight = weight + jnp.where(hit, gates_t[k : k + 1, :], 0.0)
    earlier = lax.broadcasted_iota(jnp.int32, (tokens, tokens), 0)
    later = lax.broadcasted_iota(jnp.int32, (tokens, tokens), 1)
    before = jnp.where(earlier < later, 1.0, 0.0).astype(BF)
    place = nn(named.astype(BF), before)
    place = jnp.where(named > 0.0, place, -1.0)
    slot = lax.broadcasted_iota(jnp.int32, (experts, CAP, tokens), 1).astype(F32)
    taken = place[:, None, :] == slot
    one = jnp.where(taken, 1.0, 0.0).reshape(experts * CAP, tokens)
    gate = jnp.where(taken, weight[:, None, :], 0.0).reshape(experts * CAP, tokens)
    return one, gate


def dispatch_kernel(
    routes_hbm, gates_hbm, act_hbm, up_hbm, send_hbm, routes_ref, gates_ref, act_ref, up_ref, send_ref, in_sem, out_sem
):
    experts = send_ref.shape[0]
    width = act_ref.shape[1]
    pairs = ((routes_hbm, routes_ref), (gates_hbm, gates_ref), (act_hbm, act_ref), (up_hbm, up_ref))
    loads = [pltpu.make_async_copy(source, target, in_sem.at[i]) for i, (source, target) in enumerate(pairs)]
    for load in loads:
        load.start()
    loads[0].wait()
    loads[1].wait()
    one, gate = slot_tables(routes_ref[...], gates_ref[...], experts)
    one = one.astype(BF)
    weight = jnp.sum(gate, axis=1, keepdims=True)
    loads[2].wait()
    loads[3].wait()
    step = 512
    stores = []
    for i, lo in enumerate(range(0, width, step)):
        cols = slice(lo, lo + step)
        send_ref[:, :CAP, cols] = nn(one, act_ref[:, cols]).astype(BF).reshape(experts, CAP, step)
        picked = weight * nn(one, up_ref[:, cols])
        send_ref[:, CAP:, cols] = picked.astype(BF).reshape(experts, CAP, step)
        store = pltpu.make_async_copy(send_ref.at[:, :, cols], send_hbm.at[:, :, cols], out_sem.at[i])
        store.start()
        stores.append(store)
    for store in stores:
        store.wait()


def dispatch(routes, gates, activations, upstream, experts):
    width = activations.shape[1]
    shape = (experts, 2 * CAP, width)
    return pl.pallas_call(
        dispatch_kernel,
        out_shape=pltpu.HBM(shape, BF),
        in_specs=[HBM] * 4,
        out_specs=HBM,
        scratch_shapes=[
            pltpu.VMEM(routes.shape, jnp.int32), pltpu.VMEM(gates.shape, F32), pltpu.VMEM(activations.shape, BF),
            pltpu.VMEM(upstream.shape, BF), pltpu.VMEM(shape, BF), DMA((4,)), DMA((4,)),
        ],
        compiler_params=params(12),
        name="dispatch",
    )(*(in_hbm(array) for array in (routes, gates, activations, upstream)))


def tables_kernel(routes_ref, gates_ref, table_ref):
    slots = table_ref.shape[2]
    one, gate = slot_tables(routes_ref[...], gates_ref[...], slots // CAP)
    one, gate = one.T, gate.T
    high = gate.astype(BF)
    table_ref[0] = one.astype(BF)
    table_ref[1] = high
    table_ref[2] = (gate - high.astype(F32)).astype(BF)


def tables(routes, gates, experts):
    return pl.pallas_call(
        tables_kernel,
        out_shape=jax.ShapeDtypeStruct((3, routes.shape[1], experts * CAP), BF),
        in_specs=[VMEM] * 2,
        out_specs=VMEM,
        compiler_params=params(4),
        name="tables",
    )(routes, gates)


def combine_kernel(got_ref, table_hbm, mixed_hbm, grad_hbm, table_ref, mixed_ref, grad_ref, in_sem, out_sem):
    load = pltpu.make_async_copy(table_hbm, table_ref, in_sem)
    load.start()
    experts = got_ref.shape[0]
    width = got_ref.shape[2]
    load.wait()
    one, high, low = table_ref[0], table_ref[1], table_ref[2]
    step = 512
    stores = []
    for i, lo in enumerate(range(0, width, step)):
        cols = slice(lo, lo + step)
        out = got_ref[:, :CAP, cols].reshape(experts * CAP, step)
        back = got_ref[:, CAP:, cols].reshape(experts * CAP, step)
        mixed_ref[:, cols] = (nn(high, out) + nn(low, out)).astype(BF)
        stores.append(pltpu.make_async_copy(mixed_ref.at[:, cols], mixed_hbm.at[:, cols], out_sem.at[0, i]))
        stores[-1].start()
        grad_ref[:, cols] = nn(one, back).astype(BF)
        stores.append(pltpu.make_async_copy(grad_ref.at[:, cols], grad_hbm.at[:, cols], out_sem.at[1, i]))
        stores[-1].start()
    for store in stores:
        store.wait()


def combine(got, table):
    shape = (table.shape[1], got.shape[2])
    return pl.pallas_call(
        combine_kernel,
        out_shape=(pltpu.HBM(shape, BF),) * 2,
        in_specs=[VMEM, HBM],
        out_specs=(HBM,) * 2,
        scratch_shapes=[pltpu.VMEM(table.shape, BF), pltpu.VMEM(shape, BF), pltpu.VMEM(shape, BF), DMA, DMA((2, 4))],
        compiler_params=params(8),
        name="combine",
    )(in_vmem(got), in_hbm(table))


def freeze_kernel(group_ref, *refs):
    levels, scales, frozen = refs[:3], refs[3:6], refs[-11:-8]
    level_refs, scale_refs = refs[-8:-5], refs[-5:-2]
    in_sem, out_sem = refs[-2:]

    @pl.when(group_ref[0] % 2 == FIRST_TO_FREEZE)
    def _():
        loads = [pltpu.make_async_copy(*pair, in_sem.at[i])
                 for i, pair in enumerate((*zip(scales, scale_refs), *zip(levels, level_refs)))]
        for load in loads:
            load.start()
        for load in loads[:3]:
            load.wait()
        stores = []
        for i, (level_ref, scale_ref) in enumerate(zip(level_refs, scale_refs)):
            loads[3 + i].wait()
            for j in range(scale_ref.shape[0]):
                rows = slice(j * GROUP, (j + 1) * GROUP)
                scale = scale_ref[j] if len(scale_ref.shape) == 3 else scale_ref[j : j + 1, :]
                level_ref[rows, :] = (level_ref[rows, :].astype(F32) * scale).astype(BF)
            stores.append(pltpu.make_async_copy(level_ref, frozen[i], out_sem.at[i]))
            stores[-1].start()
        for store in stores:
            store.wait()


def freeze(group, levels, scales):
    return pl.pallas_call(
        freeze_kernel,
        out_shape=tuple(pltpu.HBM(level.shape, BF) for level in levels),
        in_specs=[SMEM] + [HBM] * 6,
        out_specs=(HBM,) * 3,
        scratch_shapes=[
            *(pltpu.VMEM(level.shape, BF) for level in levels), *(pltpu.VMEM(scale.shape, F32) for scale in scales),
            DMA((6,)), DMA((3,)),
        ],
        compiler_params=params(16),
        cost_estimate=cost(1 << 24, 1 << 24),
        name="freeze",
    )(group, *(in_hbm(array) for array in (*levels, *scales)))


def expert_kernel(
    group_ref, got_ref, gate_hbm, up_hbm, down_hbm, gate_frozen_hbm, up_frozen_hbm, down_frozen_hbm,
    gate_scale_hbm, up_scale_hbm, down_scale_hbm, gate_first_hbm, up_first_hbm, down_second_hbm,
    gate_second_hbm, up_second_hbm, down_first_hbm, send_hbm, keep_hbm, other_hbm,
    gate_ref, up_ref, down_ref, gate_scale_ref, up_scale_ref, down_scale_ref, wide_ref, narrow_ref, send_ref,
    inside_ref, piece_ref, rounded_ref, level_sem, small_sem, scale_sem, out_sem, piece_sem,
):
    experts, _, width = got_ref.shape
    rows = experts * CAP
    inner = gate_ref.shape[1]
    rank = gate_first_hbm.shape[0]
    step = 256

    pairs = [(source, wide_ref.at[i * rank : (i + 1) * rank, :])
             for i, source in enumerate((gate_first_hbm, up_first_hbm, down_second_hbm))]
    pairs += [(source, narrow_ref.at[i * rank : (i + 1) * rank, :])
              for i, source in enumerate((gate_second_hbm, up_second_hbm, down_first_hbm))]
    small = [pltpu.make_async_copy(source, target, small_sem.at[i]) for i, (source, target) in enumerate(pairs)]
    for copy in small:
        copy.start()
    ready = group_ref[0] % 2 == FIRST_TO_FREEZE
    raw = ((gate_hbm, gate_ref), (up_hbm, up_ref), (down_hbm, down_ref))
    frozen = ((gate_frozen_hbm, gate_ref), (up_frozen_hbm, up_ref), (down_frozen_hbm, down_ref))
    pieces = [(part, kind) for part in range(inner // step) for kind in range(3)]

    def loads(weights, some):
        copies = []
        for part, kind in some:
            cols = slice(part * step, (part + 1) * step)
            place = (cols, slice(0, width)) if kind == 2 else (slice(0, width), cols)
            source, target = weights[kind]
            copies.append(pltpu.make_async_copy(source.at[place], target.at[place], level_sem.at[part, kind]))
        return copies

    scales = (gate_scale_ref, up_scale_ref, down_scale_ref)
    scale_loads = [pltpu.make_async_copy(source, target, scale_sem.at[i]) for i, (source, target) in enumerate(
        zip((gate_scale_hbm, up_scale_hbm, down_scale_hbm), scales))]

    @pl.when(ready)
    def _():
        for scale_ref in scales:
            scale_ref[...] = jnp.ones_like(scale_ref)

    @pl.when(jnp.logical_not(ready))
    def _():
        for copy in scale_loads:
            copy.start()

    def start(some):
        for condition, weights in ((ready, frozen), (jnp.logical_not(ready), raw)):

            @pl.when(condition)
            def _(weights=weights):
                for copy in loads(weights, some):
                    copy.start()

    start(pieces[:3])

    def land(part):
        for copy in loads(raw, pieces[3 * part : 3 * part + 3]):
            copy.wait()

        cols = slice(part * step, (part + 1) * step)
        for target, scale_ref in ((gate_ref, gate_scale_ref), (up_ref, up_scale_ref)):
            for i in range(width // GROUP):
                group = slice(i * GROUP, (i + 1) * GROUP)
                target[group, cols] = (target[group, cols].astype(F32) * scale_ref[i : i + 1, cols]).astype(BF)
        for i in range(part * step // GROUP, (part + 1) * step // GROUP):
            group = slice(i * GROUP, (i + 1) * GROUP)
            down_ref[group, :] = (down_ref[group, :].astype(F32) * down_scale_ref[i]).astype(BF)

    x = got_ref[:, :CAP, :].reshape(rows, width)
    g = got_ref[:, CAP:, :].reshape(rows, width)
    first_ref = wide_ref.at[: 2 * rank, :]
    down_second_ref = wide_ref.at[2 * rank :, :]
    gate_second_ref = narrow_ref.at[:rank, :]
    up_second_ref = narrow_ref.at[rank : 2 * rank, :]
    down_first_ref = narrow_ref.at[2 * rank :, :]
    for copy in small:
        copy.wait()
    start(pieces[3:])

    @pl.when(jnp.logical_not(ready))
    def _():
        for copy in scale_loads:
            copy.wait()

    first_low = nt(x, first_ref[...]).astype(BF)
    gate_low, up_low = first_low[:, :rank], first_low[:, rank:]
    back_down = nt(g, down_second_ref[...]).astype(BF)
    half = jnp.asarray(SCALING, BF)
    down_low = jnp.zeros((rows, rank), F32)
    back_gate = jnp.zeros((rows, rank), F32)
    back_up = jnp.zeros((rows, rank), F32)
    for index, (part, kind) in enumerate(pieces):
        if kind == 0:
            land(part)
        cols = slice(part * step, (part + 1) * step)
        if kind == 0:
            gate_pre = nn(x, gate_ref[:, cols]) + nn(gate_low * half, gate_second_ref[:, cols])
            logistic = jax.nn.sigmoid(gate_pre)
            activated = gate_pre * logistic
            slope = logistic * (1.0 + gate_pre * (1.0 - logistic))
        elif kind == 1:
            up_pre = nn(x, up_ref[:, cols]) + nn(up_low * half, up_second_ref[:, cols])
            hidden = (activated * up_pre).astype(BF)
            inside_ref[0, :, cols] = hidden
            down_low += nt(hidden, down_first_ref[:, cols])
        else:
            d_hidden = nt(g, down_ref[cols, :]) + nn(back_down * half, down_first_ref[:, cols])
            d_gate = (d_hidden * up_pre * slope).astype(BF)
            d_up = (d_hidden * activated).astype(BF)
            inside_ref[1, :, cols] = d_gate
            inside_ref[2, :, cols] = d_up
            back_gate += nt(d_gate, gate_second_ref[:, cols])
            back_up += nt(d_up, up_second_ref[:, cols])
    down_low = down_low.astype(BF)
    back_both = jnp.concatenate([back_gate, back_up], axis=1).astype(BF)
    hidden, d_gate, d_up = inside_ref[0], inside_ref[1], inside_ref[2]
    stores = []
    for i, lo in enumerate(range(0, width, step)):
        cols = slice(lo, lo + step)
        out = nn(hidden, down_ref[:, cols]) + nn(down_low * half, down_second_ref[:, cols])
        send_ref[:, :CAP, cols] = out.astype(BF).reshape(experts, CAP, step)
        back = nt(d_gate, gate_ref[cols, :]) + nt(d_up, up_ref[cols, :])
        back = back + nn(back_both * half, first_ref[:, cols])
        send_ref[:, CAP:, cols] = back.astype(BF).reshape(experts, CAP, step)
        if lo + step in SPLITS:
            cols = slice(lo + step - SPLITS[lo + step], lo + step)
            stores.append(pltpu.make_async_copy(send_ref.at[:, :, cols], send_hbm.at[:, :, cols], out_sem.at[i]))
            stores[-1].start()
    groups = piece_ref.shape[0]
    column = width // groups
    for lo in range(0, width, 512):
        cols = slice(lo, lo + 512)
        both = SCALING * tn(back_both, got_ref[:, :CAP, cols].reshape(rows, 512))
        down = SCALING * tn(down_low, got_ref[:, CAP:, cols].reshape(rows, 512))
        for i in range(512 // column):
            part = slice(i * column, (i + 1) * column)
            piece_ref[lo // column + i, : 2 * rank, :] = both[:, part]
            piece_ref[lo // column + i, 2 * rank : 3 * rank, :] = down[:, part]
    source = lax.broadcasted_iota(jnp.int32, (rank, 8 * rank), 0)
    target = lax.broadcasted_iota(jnp.int32, (rank, 8 * rank), 1)
    narrow = jnp.zeros((8 * rank, inner), F32)
    for i, (left, right) in enumerate(((gate_low, d_gate), (up_low, d_up), (back_down, hidden))):
        spread = jnp.where(target == 8 * source + i, SCALING, 0.0).astype(BF)
        narrow += tn(nn(left, spread).astype(BF), right)
    for piece in range(groups):
        for i in range(inner // column):
            at = 3 * rank + 8 * i
            piece_ref[piece, at : at + 8, :] = narrow[8 * piece : 8 * piece + 8, i * column : (i + 1) * column]
    group = group_ref[0]
    side = group % 2
    plane = group // 2
    rounded_ref[...] = piece_ref[...].astype(BF)
    half = groups // 4
    for place in range(groups // 2):
        turned = (place & 1) * 4 + (place & 2) + (place >> 2)
        other = lax.bitwise_xor(plane, jnp.int32(turned))
        source, target = (piece_ref, keep_hbm) if place < half else (rounded_ref, other_hbm)
        for i, core in enumerate((side, 1 - side)):
            copy = pltpu.make_async_copy(
                source.at[2 * other + core], target.at[place % half, i], piece_sem.at[place, i]
            )
            stores.append(copy)
            copy.start()
    for store in stores:
        store.wait()


def expert(group, groups, got, levels, frozen, scales, wide, narrow):
    rows = got.shape[0] * CAP
    width = got.shape[2]
    inner = levels[0].shape[1]
    rank = wide[0].shape[0]
    column = width // groups
    height = 3 * rank + 8 * (inner // column)
    part = (groups // 4, 2, height, column)
    return pl.pallas_call(
        expert_kernel,
        out_shape=(pltpu.HBM(got.shape, BF), pltpu.HBM(part, F32), pltpu.HBM(part, BF)),
        in_specs=[SMEM, VMEM] + [HBM] * 15,
        out_specs=(HBM,) * 3,
        scratch_shapes=[
            *(pltpu.VMEM(level.shape, BF) for level in levels),
            *(pltpu.VMEM(scale.shape, F32) for scale in scales),
            pltpu.VMEM((3 * rank, width), BF), pltpu.VMEM((3 * rank, inner), BF),
            pltpu.VMEM(got.shape, BF), pltpu.VMEM((3, rows, inner), BF), pltpu.VMEM((groups, height, column), F32),
            pltpu.VMEM((groups, height, column), BF),
            DMA((inner // 256, 3)), DMA((6,)), DMA((3,)), DMA((width // 256,)), DMA((groups // 2, 2)),
        ],
        compiler_params=params(32),
        name="expert",
    )(group, in_vmem(got), *(in_hbm(array) for array in (*levels, *frozen, *scales, *wide, *narrow)))


def shards(
    activations, routes, gates, gate_levels, gate_scales, up_levels, up_scales, down_levels, down_scales,
    gate_adapter_first, gate_adapter_second, up_adapter_first, up_adapter_second,
    down_adapter_first, down_adapter_second, upstream,
):
    experts = lax.axis_size("expert")
    groups = lax.axis_size("dp")
    width = activations.shape[1]
    inner = gate_levels.shape[2]
    rank = gate_adapter_first.shape[1]

    routes, gates = routes.T, gates.T
    group = lax.axis_index("dp").astype(jnp.int32).reshape(1)
    levels = (gate_levels[0], up_levels[0], down_levels[0])
    scales = (gate_scales[0], up_scales[0], down_scales.transpose(1, 0, 2))
    frozen = freeze(group, levels, scales)
    routes, gates, frozen = lax.optimization_barrier((routes, gates, frozen))
    send = dispatch(routes, gates, activations, upstream, experts)
    send, group, frozen = lax.optimization_barrier((send, group, frozen))
    got = lax.all_to_all(send, "expert", split_axis=0, concat_axis=0, tiled=True)

    send, keep, other = expert(
        group,
        groups,
        got,
        levels,
        frozen,
        scales,
        (gate_adapter_first[0], up_adapter_first[0], down_adapter_second[0]),
        (gate_adapter_second[0], up_adapter_second[0], down_adapter_first[0]),
    )
    routes, gates, keep = lax.optimization_barrier((routes, gates, keep))
    table = tables(routes, gates, experts)
    back = lax.all_to_all(send, "expert", split_axis=0, concat_axis=0, tiled=True)

    def swap(part, mask):
        return lax.ppermute(part, "dp", [(i, i ^ mask) for i in range(groups)])

    total = keep + swap(other, 2).astype(F32)
    sent = total.astype(BF)
    total = total[0] + (swap(sent[1], 8).astype(F32) + swap(sent[2], 4).astype(F32) + swap(sent[3], 12).astype(F32))
    total = total[0] + swap(total[1], 1)
    column = width // groups
    grad_wide = total[: 3 * rank].reshape(1, 3, rank, column)
    narrow = total[3 * rank :].reshape(inner // column, 8, column)[:, :3]
    grad_narrow = narrow.transpose(1, 0, 2).reshape(1, 3, 1, inner)

    mixed, input_grad = combine(back, table)
    return mixed, input_grad, grad_wide, grad_narrow


def solution(mesh):
    rows = P(("dp", "expert"), None)
    weight = P("expert", None, None)
    return jax.shard_map(
        shards,
        mesh=mesh,
        in_specs=(rows,) * 3 + (weight,) * 12 + (rows,),
        out_specs=(rows, rows, P("expert", None, None, "dp"), P("expert", None, "dp", None)),
        check_vma=False,
    )
```

```python
import jax
import jax.numpy as jnp
from jax import lax
from jax.experimental import pallas as pl
from jax.experimental.pallas import tpu as pltpu
from jax.sharding import PartitionSpec as P

GROUP = 128
FIRST_TO_FREEZE = 0
SPLIT = (0,)
CAP = 16
SCALING = 0.5
BF = jnp.bfloat16
F32 = jnp.float32
VMEM = pl.BlockSpec(memory_space=pltpu.VMEM)
SMEM = pl.BlockSpec(memory_space=pltpu.SMEM)
HBM = pl.BlockSpec(memory_space=pltpu.HBM)
DMA = pltpu.SemaphoreType.DMA
SPLITS = {1280: 1280, 2048: 768}


def nn(a, b):
    return lax.dot_general(a, b, (((1,), (0,)), ((), ())), preferred_element_type=F32)


def nt(a, b):
    return lax.dot_general(a, b, (((1,), (1,)), ((), ())), preferred_element_type=F32)


def tn(a, b):
    return lax.dot_general(a, b, (((0,), (0,)), ((), ())), preferred_element_type=F32)


def params(mebibytes):
    return pltpu.CompilerParams(vmem_limit_bytes=mebibytes * 1024 * 1024)


def cost(flops, bytes_accessed):
    return pl.CostEstimate(flops=flops, bytes_accessed=bytes_accessed, transcendentals=0)


def in_vmem(array):
    return pltpu.with_memory_space_constraint(array, pltpu.VMEM)


def in_hbm(array):
    return pltpu.with_memory_space_constraint(array, pltpu.HBM)


def slot_tables(routes, gates_t, experts):
    top, tokens = routes.shape
    routes_t = routes.astype(F32)
    column = lax.broadcasted_iota(jnp.int32, (experts, tokens), 0).astype(F32)
    named = jnp.zeros((experts, tokens), F32)
    weight = jnp.zeros((experts, tokens), F32)
    for k in range(top):
        hit = routes_t[k : k + 1, :] == column
        named = named + jnp.where(hit, 1.0, 0.0)
        weight = weight + jnp.where(hit, gates_t[k : k + 1, :], 0.0)
    earlier = lax.broadcasted_iota(jnp.int32, (tokens, tokens), 0)
    later = lax.broadcasted_iota(jnp.int32, (tokens, tokens), 1)
    before = jnp.where(earlier < later, 1.0, 0.0).astype(BF)
    place = nn(named.astype(BF), before)
    place = jnp.where(named > 0.0, place, -1.0)
    slot = lax.broadcasted_iota(jnp.int32, (experts, CAP, tokens), 1).astype(F32)
    taken = place[:, None, :] == slot
    one = jnp.where(taken, 1.0, 0.0).reshape(experts * CAP, tokens)
    gate = jnp.where(taken, weight[:, None, :], 0.0).reshape(experts * CAP, tokens)
    return one, gate


def dispatch_kernel(
    routes_hbm, gates_hbm, act_hbm, up_hbm, send_hbm, routes_ref, gates_ref, act_ref, up_ref, send_ref, in_sem, out_sem
):
    experts = send_ref.shape[0]
    width = act_ref.shape[1]
    pairs = ((routes_hbm, routes_ref), (gates_hbm, gates_ref), (act_hbm, act_ref), (up_hbm, up_ref))
    loads = [pltpu.make_async_copy(source, target, in_sem.at[i]) for i, (source, target) in enumerate(pairs)]
    for load in loads:
        load.start()
    loads[0].wait()
    loads[1].wait()
    one, gate = slot_tables(routes_ref[...], gates_ref[...], experts)
    one = one.astype(BF)
    weight = jnp.sum(gate, axis=1, keepdims=True)
    loads[2].wait()
    loads[3].wait()
    step = 512
    stores = []
    for i, lo in enumerate(range(0, width, step)):
        cols = slice(lo, lo + step)
        send_ref[:, :CAP, cols] = nn(one, act_ref[:, cols]).astype(BF).reshape(experts, CAP, step)
        picked = weight * nn(one, up_ref[:, cols])
        send_ref[:, CAP:, cols] = picked.astype(BF).reshape(experts, CAP, step)
        store = pltpu.make_async_copy(send_ref.at[:, :, cols], send_hbm.at[:, :, cols], out_sem.at[i])
        store.start()
        stores.append(store)
    for store in stores:
        store.wait()


def dispatch(routes, gates, activations, upstream, experts):
    width = activations.shape[1]
    shape = (experts, 2 * CAP, width)
    return pl.pallas_call(
        dispatch_kernel,
        out_shape=pltpu.HBM(shape, BF),
        in_specs=[HBM] * 4,
        out_specs=HBM,
        scratch_shapes=[
            pltpu.VMEM(routes.shape, jnp.int32), pltpu.VMEM(gates.shape, F32), pltpu.VMEM(activations.shape, BF),
            pltpu.VMEM(upstream.shape, BF), pltpu.VMEM(shape, BF), DMA((4,)), DMA((4,)),
        ],
        compiler_params=params(12),
        name="dispatch",
    )(*(in_hbm(array) for array in (routes, gates, activations, upstream)))


def tables_kernel(routes_ref, gates_ref, table_ref):
    slots = table_ref.shape[2]
    one, gate = slot_tables(routes_ref[...], gates_ref[...], slots // CAP)
    one, gate = one.T, gate.T
    high = gate.astype(BF)
    table_ref[0] = one.astype(BF)
    table_ref[1] = high
    table_ref[2] = (gate - high.astype(F32)).astype(BF)


def tables(routes, gates, experts):
    return pl.pallas_call(
        tables_kernel,
        out_shape=jax.ShapeDtypeStruct((3, routes.shape[1], experts * CAP), BF),
        in_specs=[VMEM] * 2,
        out_specs=VMEM,
        compiler_params=params(4),
        name="tables",
    )(routes, gates)


def combine_kernel(
    got_ref, table_hbm, mine_ref, theirs_ref, mixed_hbm, grad_hbm, wide_hbm, narrow_hbm, table_ref, wide_ref, narrow_ref,
    mixed_ref, grad_ref, in_sem, out_sem, wide_sem,
):
    load = pltpu.make_async_copy(table_hbm, table_ref, in_sem)
    load.start()
    total = mine_ref[...] + theirs_ref[...]
    tall, column = wide_ref.shape
    wide_ref[...] = total[:tall]
    for i in range(narrow_ref.shape[2] // column):
        for j in range(narrow_ref.shape[0]):
            at = tall + 8 * i + j
            narrow_ref[j, :, i * column : (i + 1) * column] = total[at : at + 1]
    stores = [
        pltpu.make_async_copy(wide_ref, wide_hbm, wide_sem.at[0]),
        pltpu.make_async_copy(narrow_ref, narrow_hbm, wide_sem.at[1]),
    ]
    for store in stores:
        store.start()
    experts = got_ref.shape[0]
    width = got_ref.shape[2]
    load.wait()
    one, high, low = table_ref[0], table_ref[1], table_ref[2]
    step = 512
    for i, lo in enumerate(range(0, width, step)):
        cols = slice(lo, lo + step)
        out = got_ref[:, :CAP, cols].reshape(experts * CAP, step)
        back = got_ref[:, CAP:, cols].reshape(experts * CAP, step)
        mixed_ref[:, cols] = (nn(high, out) + nn(low, out)).astype(BF)
        stores.append(pltpu.make_async_copy(mixed_ref.at[:, cols], mixed_hbm.at[:, cols], out_sem.at[0, i]))
        stores[-1].start()
        grad_ref[:, cols] = nn(one, back).astype(BF)
        stores.append(pltpu.make_async_copy(grad_ref.at[:, cols], grad_hbm.at[:, cols], out_sem.at[1, i]))
        stores[-1].start()
    for store in stores:
        store.wait()


def combine(got, table, mine, theirs, tall, inner):
    shape = (table.shape[1], got.shape[2])
    wide, narrow = (tall, mine.shape[1]), (3, 1, inner)
    return pl.pallas_call(
        combine_kernel,
        out_shape=(pltpu.HBM(shape, BF), pltpu.HBM(shape, BF), pltpu.HBM(wide, F32), pltpu.HBM(narrow, F32)),
        in_specs=[VMEM, HBM, VMEM, VMEM],
        out_specs=(HBM,) * 4,
        scratch_shapes=[
            pltpu.VMEM(table.shape, BF), pltpu.VMEM(wide, F32), pltpu.VMEM(narrow, F32), pltpu.VMEM(shape, BF),
            pltpu.VMEM(shape, BF), DMA, DMA((2, 4)), DMA((2,)),
        ],
        compiler_params=params(8),
        name="combine",
    )(in_vmem(got), in_hbm(table), mine, theirs)


def freeze_kernel(group_ref, *refs):
    levels, scales, frozen = refs[:3], refs[3:6], refs[-11:-8]
    level_refs, scale_refs = refs[-8:-5], refs[-5:-2]
    in_sem, out_sem = refs[-2:]

    @pl.when(group_ref[0] % 2 == FIRST_TO_FREEZE)
    def _():
        loads = [pltpu.make_async_copy(*pair, in_sem.at[i])
                 for i, pair in enumerate((*zip(scales, scale_refs), *zip(levels, level_refs)))]
        for load in loads:
            load.start()
        for load in loads[:3]:
            load.wait()
        stores = []
        for i, (level_ref, scale_ref) in enumerate(zip(level_refs, scale_refs)):
            loads[3 + i].wait()
            for j in range(scale_ref.shape[0]):
                rows = slice(j * GROUP, (j + 1) * GROUP)
                scale = scale_ref[j] if len(scale_ref.shape) == 3 else scale_ref[j : j + 1, :]
                level_ref[rows, :] = (level_ref[rows, :].astype(F32) * scale).astype(BF)
            stores.append(pltpu.make_async_copy(level_ref, frozen[i], out_sem.at[i]))
            stores[-1].start()
        for store in stores:
            store.wait()


def freeze(group, levels, scales):
    return pl.pallas_call(
        freeze_kernel,
        out_shape=tuple(pltpu.HBM(level.shape, BF) for level in levels),
        in_specs=[SMEM] + [HBM] * 6,
        out_specs=(HBM,) * 3,
        scratch_shapes=[
            *(pltpu.VMEM(level.shape, BF) for level in levels), *(pltpu.VMEM(scale.shape, F32) for scale in scales),
            DMA((6,)), DMA((3,)),
        ],
        compiler_params=params(16),
        cost_estimate=cost(1 << 24, 1 << 24),
        name="freeze",
    )(group, *(in_hbm(array) for array in (*levels, *scales)))


def expert_kernel(
    group_ref, got_ref, gate_hbm, up_hbm, down_hbm, gate_frozen_hbm, up_frozen_hbm, down_frozen_hbm,
    gate_scale_hbm, up_scale_hbm, down_scale_hbm, gate_first_hbm, up_first_hbm, down_second_hbm,
    gate_second_hbm, up_second_hbm, down_first_hbm, send_hbm, keep_hbm, other_hbm,
    gate_ref, up_ref, down_ref, gate_scale_ref, up_scale_ref, down_scale_ref, wide_ref, narrow_ref, send_ref,
    inside_ref, piece_ref, rounded_ref, level_sem, small_sem, scale_sem, out_sem, piece_sem,
):
    experts, _, width = got_ref.shape
    rows = experts * CAP
    inner = gate_ref.shape[1]
    rank = gate_first_hbm.shape[0]
    step = 256

    pairs = [(source, wide_ref.at[i * rank : (i + 1) * rank, :])
             for i, source in enumerate((gate_first_hbm, up_first_hbm, down_second_hbm))]
    pairs += [(down_second_hbm, down_ref.at[inner : inner + rank, :])]
    pairs += [(source, narrow_ref.at[i * rank : (i + 1) * rank, :])
              for i, source in enumerate((gate_second_hbm, up_second_hbm, down_first_hbm))]
    small = [pltpu.make_async_copy(source, target, small_sem.at[i]) for i, (source, target) in enumerate(pairs)]
    for copy in small:
        copy.start()
    ready = group_ref[0] % 2 == FIRST_TO_FREEZE
    raw = ((gate_hbm, gate_ref), (up_hbm, up_ref), (down_hbm, down_ref))
    frozen = ((gate_frozen_hbm, gate_ref), (up_frozen_hbm, up_ref), (down_frozen_hbm, down_ref))
    pieces = [(part, kind) for part in range(inner // step) for kind in range(3)]

    def loads(weights, some):
        copies = []
        for part, kind in some:
            cols = slice(part * step, (part + 1) * step)
            place = (cols, slice(0, width)) if kind == 2 else (slice(0, width), cols)
            source, target = weights[kind]
            copies.append(pltpu.make_async_copy(source.at[place], target.at[place], level_sem.at[part, kind]))
        return copies

    scales = (gate_scale_ref, up_scale_ref, down_scale_ref)
    scale_loads = [pltpu.make_async_copy(source, target, scale_sem.at[i]) for i, (source, target) in enumerate(
        zip((gate_scale_hbm, up_scale_hbm, down_scale_hbm), scales))]

    @pl.when(ready)
    def _():
        for scale_ref in scales:
            scale_ref[...] = jnp.ones_like(scale_ref)

    @pl.when(jnp.logical_not(ready))
    def _():
        for copy in scale_loads:
            copy.start()

    def start(some):
        for condition, weights in ((ready, frozen), (jnp.logical_not(ready), raw)):

            @pl.when(condition)
            def _(weights=weights):
                for copy in loads(weights, some):
                    copy.start()

    start(pieces[:2])
    down_ref[inner + rank :, :] = jnp.zeros((GROUP - rank, width), BF)

    def land(part, kinds=(0, 1, 2)):
        for copy in loads(raw, [(part, kind) for kind in kinds]):
            copy.wait()

        cols = slice(part * step, (part + 1) * step)
        for target, scale_ref in ((gate_ref, gate_scale_ref), (up_ref, up_scale_ref)) if 0 in kinds else ():
            for i in range(width // GROUP):
                group = slice(i * GROUP, (i + 1) * GROUP)
                target[group, cols] = (target[group, cols].astype(F32) * scale_ref[i : i + 1, cols]).astype(BF)
        for i in range(part * step // GROUP, (part + 1) * step // GROUP) if 2 in kinds else ():
            group = slice(i * GROUP, (i + 1) * GROUP)
            down_ref[group, :] = (down_ref[group, :].astype(F32) * down_scale_ref[i]).astype(BF)

    x = got_ref[:, :CAP, :].reshape(rows, width)
    g = got_ref[:, CAP:, :].reshape(rows, width)
    first_ref = wide_ref.at[: 2 * rank, :]
    down_second_ref = wide_ref.at[2 * rank :, :]
    gate_second_ref = narrow_ref.at[:rank, :]
    up_second_ref = narrow_ref.at[rank : 2 * rank, :]
    down_first_ref = narrow_ref.at[2 * rank :, :]
    for copy in small:
        copy.wait()
    start(pieces[2:])

    @pl.when(jnp.logical_not(ready))
    def _():
        for copy in scale_loads:
            copy.wait()

    first_low = nt(x, first_ref[...]).astype(BF)
    gate_low, up_low = first_low[:, :rank], first_low[:, rank:]
    back_down = nt(g, down_second_ref[...]).astype(BF)
    half = jnp.asarray(SCALING, BF)
    down_low = jnp.zeros((rows, rank), F32)
    back_gate = jnp.zeros((rows, rank), F32)
    back_up = jnp.zeros((rows, rank), F32)
    for index, (part, kind) in enumerate(pieces):
        if kind == 0:
            land(part, (0, 1) if part in SPLIT else (0, 1, 2))
        if kind == 2 and part in SPLIT:
            land(part, (2,))
        cols = slice(part * step, (part + 1) * step)
        if kind == 0:
            gate_pre = nn(x, gate_ref[:, cols]) + nn(gate_low * half, gate_second_ref[:, cols])
            logistic = jax.nn.sigmoid(gate_pre)
            activated = gate_pre * logistic
            slope = logistic * (1.0 + gate_pre * (1.0 - logistic))
        elif kind == 1:
            up_pre = nn(x, up_ref[:, cols]) + nn(up_low * half, up_second_ref[:, cols])
            hidden = (activated * up_pre).astype(BF)
            inside_ref[0, :, cols] = hidden
            down_low += nt(hidden, down_first_ref[:, cols])
        else:
            d_hidden = nt(g, down_ref[cols, :]) + nn(back_down * half, down_first_ref[:, cols])
            d_gate = (d_hidden * up_pre * slope).astype(BF)
            d_up = (d_hidden * activated).astype(BF)
            inside_ref[1, :, cols] = d_gate
            inside_ref[2, :, cols] = d_up
            back_gate += nt(d_gate, gate_second_ref[:, cols])
            back_up += nt(d_up, up_second_ref[:, cols])
    down_low = down_low.astype(BF)
    back_both = jnp.concatenate([back_gate, back_up], axis=1).astype(BF)
    hidden, d_gate, d_up = inside_ref[0], inside_ref[1], inside_ref[2]
    hidden_low = jnp.concatenate([hidden, down_low * half, jnp.zeros((rows, GROUP - rank), BF)], axis=1)
    stores = []
    for i, lo in enumerate(range(0, width, step)):
        cols = slice(lo, lo + step)
        out = nn(hidden_low, down_ref[:, cols])
        send_ref[:, :CAP, cols] = out.astype(BF).reshape(experts, CAP, step)
        back = nt(d_gate, gate_ref[cols, :]) + nt(d_up, up_ref[cols, :])
        back = back + nn(back_both * half, first_ref[:, cols])
        send_ref[:, CAP:, cols] = back.astype(BF).reshape(experts, CAP, step)
        if lo + step in SPLITS:
            cols = slice(lo + step - SPLITS[lo + step], lo + step)
            stores.append(pltpu.make_async_copy(send_ref.at[:, :, cols], send_hbm.at[:, :, cols], out_sem.at[i]))
            stores[-1].start()
    groups = piece_ref.shape[0]
    column = width // groups
    for lo in range(0, width, 512):
        cols = slice(lo, lo + 512)
        both = SCALING * tn(back_both, got_ref[:, :CAP, cols].reshape(rows, 512))
        down = SCALING * tn(down_low, got_ref[:, CAP:, cols].reshape(rows, 512))
        for i in range(512 // column):
            part = slice(i * column, (i + 1) * column)
            piece_ref[lo // column + i, : 2 * rank, :] = both[:, part]
            piece_ref[lo // column + i, 2 * rank : 3 * rank, :] = down[:, part]
    source = lax.broadcasted_iota(jnp.int32, (rank, 8 * rank), 0)
    target = lax.broadcasted_iota(jnp.int32, (rank, 8 * rank), 1)
    narrow = jnp.zeros((8 * rank, inner), F32)
    for i, (left, right) in enumerate(((gate_low, d_gate), (up_low, d_up), (back_down, hidden))):
        spread = jnp.where(target == 8 * source + i, SCALING, 0.0).astype(BF)
        narrow += tn(nn(left, spread).astype(BF), right)
    for piece in range(groups):
        for i in range(inner // column):
            at = 3 * rank + 8 * i
            piece_ref[piece, at : at + 8, :] = narrow[8 * piece : 8 * piece + 8, i * column : (i + 1) * column]
    group = group_ref[0]
    side = group % 2
    plane = group // 2
    rounded_ref[...] = piece_ref[...].astype(BF)
    half = groups // 4
    for place in range(groups // 2):
        turned = (place & 1) * 4 + (place & 2) + (place >> 2)
        other = lax.bitwise_xor(plane, jnp.int32(turned))
        source, target = (piece_ref, keep_hbm) if place < half else (rounded_ref, other_hbm)
        for i, core in enumerate((side, 1 - side)):
            copy = pltpu.make_async_copy(
                source.at[2 * other + core], target.at[place % half, i], piece_sem.at[place, i]
            )
            stores.append(copy)
            copy.start()
    for store in stores:
        store.wait()


def expert(group, groups, got, levels, frozen, scales, wide, narrow):
    rows = got.shape[0] * CAP
    width = got.shape[2]
    inner = levels[0].shape[1]
    rank = wide[0].shape[0]
    column = width // groups
    height = 3 * rank + 8 * (inner // column)
    part = (groups // 4, 2, height, column)
    return pl.pallas_call(
        expert_kernel,
        out_shape=(pltpu.HBM(got.shape, BF), pltpu.HBM(part, F32), pltpu.HBM(part, BF)),
        in_specs=[SMEM, VMEM] + [HBM] * 15,
        out_specs=(HBM,) * 3,
        scratch_shapes=[
            pltpu.VMEM(levels[0].shape, BF), pltpu.VMEM(levels[1].shape, BF), pltpu.VMEM((inner + GROUP, width), BF),
            *(pltpu.VMEM(scale.shape, F32) for scale in scales),
            pltpu.VMEM((3 * rank, width), BF), pltpu.VMEM((3 * rank, inner), BF),
            pltpu.VMEM(got.shape, BF), pltpu.VMEM((3, rows, inner), BF), pltpu.VMEM((groups, height, column), F32),
            pltpu.VMEM((groups, height, column), BF),
            DMA((inner // 256, 3)), DMA((7,)), DMA((3,)), DMA((width // 256,)), DMA((groups // 2, 2)),
        ],
        compiler_params=params(32),
        name="expert",
    )(group, in_vmem(got), *(in_hbm(array) for array in (*levels, *frozen, *scales, *wide, *narrow)))


def shards(
    activations, routes, gates, gate_levels, gate_scales, up_levels, up_scales, down_levels, down_scales,
    gate_adapter_first, gate_adapter_second, up_adapter_first, up_adapter_second,
    down_adapter_first, down_adapter_second, upstream,
):
    experts = lax.axis_size("expert")
    groups = lax.axis_size("dp")
    width = activations.shape[1]
    inner = gate_levels.shape[2]
    rank = gate_adapter_first.shape[1]

    routes, gates = routes.T, gates.T
    group = lax.axis_index("dp").astype(jnp.int32).reshape(1)
    levels = (gate_levels[0], up_levels[0], down_levels[0])
    scales = (gate_scales[0], up_scales[0], down_scales.transpose(1, 0, 2))
    frozen = freeze(group, levels, scales)
    routes, gates, frozen = lax.optimization_barrier((routes, gates, frozen))
    send = dispatch(routes, gates, activations, upstream, experts)
    send, group, frozen = lax.optimization_barrier((send, group, frozen))
    got = lax.all_to_all(send, "expert", split_axis=0, concat_axis=0, tiled=True)

    send, keep, other = expert(
        group,
        groups,
        got,
        levels,
        frozen,
        scales,
        (gate_adapter_first[0], up_adapter_first[0], down_adapter_second[0]),
        (gate_adapter_second[0], up_adapter_second[0], down_adapter_first[0]),
    )
    routes, gates, keep = lax.optimization_barrier((routes, gates, keep))
    table = tables(routes, gates, experts)
    back = lax.all_to_all(send, "expert", split_axis=0, concat_axis=0, tiled=True)

    def swap(part, mask):
        return lax.ppermute(part, "dp", [(i, i ^ mask) for i in range(groups)])

    total = keep + swap(other, 2).astype(F32)
    sent = total.astype(BF)
    total = total[0] + (swap(sent[1], 8).astype(F32) + swap(sent[2], 4).astype(F32) + swap(sent[3], 12).astype(F32))
    mixed, input_grad, grad_wide, grad_narrow = combine(back, table, total[0], swap(total[1], 1), 3 * rank, inner)
    grad_wide = grad_wide.reshape(1, 3, rank, width // groups)
    grad_narrow = grad_narrow.reshape(1, 3, 1, inner)
    return mixed, input_grad, grad_wide, grad_narrow


def solution(mesh):
    rows = P(("dp", "expert"), None)
    weight = P("expert", None, None)
    return jax.shard_map(
        shards,
        mesh=mesh,
        in_specs=(rows,) * 3 + (weight,) * 12 + (rows,),
        out_specs=(rows, rows, P("expert", None, None, "dp"), P("expert", None, "dp", None)),
        check_vma=False,
    )
```

```python
import jax
import jax.numpy as jnp
from jax import lax
from jax.experimental import pallas as pl
from jax.experimental.pallas import tpu as pltpu
from jax.sharding import PartitionSpec as P

GROUP = 128
FIRST_TO_FREEZE = 0
SPLIT = (0,)
CAP = 16
SCALING = 0.5
BF = jnp.bfloat16
F32 = jnp.float32
VMEM = pl.BlockSpec(memory_space=pltpu.VMEM)
SMEM = pl.BlockSpec(memory_space=pltpu.SMEM)
HBM = pl.BlockSpec(memory_space=pltpu.HBM)
DMA = pltpu.SemaphoreType.DMA
SPLITS = {1280: 1280, 2048: 768}


def nn(a, b):
    return lax.dot_general(a, b, (((1,), (0,)), ((), ())), preferred_element_type=F32)


def nt(a, b):
    return lax.dot_general(a, b, (((1,), (1,)), ((), ())), preferred_element_type=F32)


def tn(a, b):
    return lax.dot_general(a, b, (((0,), (0,)), ((), ())), preferred_element_type=F32)


def params(mebibytes):
    return pltpu.CompilerParams(vmem_limit_bytes=mebibytes * 1024 * 1024)


def cost(flops, bytes_accessed):
    return pl.CostEstimate(flops=flops, bytes_accessed=bytes_accessed, transcendentals=0)


def in_vmem(array):
    return pltpu.with_memory_space_constraint(array, pltpu.VMEM)


def in_hbm(array):
    return pltpu.with_memory_space_constraint(array, pltpu.HBM)


def slot_tables(routes, gates_t, experts):
    top, tokens = routes.shape
    routes_t = routes.astype(F32)
    column = lax.broadcasted_iota(jnp.int32, (experts, tokens), 0).astype(F32)
    named = jnp.zeros((experts, tokens), F32)
    weight = jnp.zeros((experts, tokens), F32)
    for k in range(top):
        hit = routes_t[k : k + 1, :] == column
        named = named + jnp.where(hit, 1.0, 0.0)
        weight = weight + jnp.where(hit, gates_t[k : k + 1, :], 0.0)
    earlier = lax.broadcasted_iota(jnp.int32, (tokens, tokens), 0)
    later = lax.broadcasted_iota(jnp.int32, (tokens, tokens), 1)
    before = jnp.where(earlier < later, 1.0, 0.0).astype(BF)
    place = nn(named.astype(BF), before)
    place = jnp.where(named > 0.0, place, -1.0)
    slot = lax.broadcasted_iota(jnp.int32, (experts, CAP, tokens), 1).astype(F32)
    taken = place[:, None, :] == slot
    one = jnp.where(taken, 1.0, 0.0).reshape(experts * CAP, tokens)
    gate = jnp.where(taken, weight[:, None, :], 0.0).reshape(experts * CAP, tokens)
    return one, gate


def dispatch_kernel(
    routes_hbm, gates_hbm, act_hbm, up_hbm, send_hbm, routes_ref, gates_ref, act_ref, up_ref, send_ref, in_sem, out_sem
):
    experts = send_ref.shape[0]
    width = act_ref.shape[1]
    pairs = ((routes_hbm, routes_ref), (gates_hbm, gates_ref), (act_hbm, act_ref), (up_hbm, up_ref))
    loads = [pltpu.make_async_copy(source, target, in_sem.at[i]) for i, (source, target) in enumerate(pairs)]
    for load in loads:
        load.start()
    loads[0].wait()
    loads[1].wait()
    one, gate = slot_tables(routes_ref[...], gates_ref[...], experts)
    one = one.astype(BF)
    weight = jnp.sum(gate, axis=1, keepdims=True)
    loads[2].wait()
    loads[3].wait()
    step = 512
    stores = []
    for i, lo in enumerate(range(0, width, step)):
        cols = slice(lo, lo + step)
        send_ref[:, :CAP, cols] = nn(one, act_ref[:, cols]).astype(BF).reshape(experts, CAP, step)
        picked = weight * nn(one, up_ref[:, cols])
        send_ref[:, CAP:, cols] = picked.astype(BF).reshape(experts, CAP, step)
        store = pltpu.make_async_copy(send_ref.at[:, :, cols], send_hbm.at[:, :, cols], out_sem.at[i])
        store.start()
        stores.append(store)
    for store in stores:
        store.wait()


def dispatch(routes, gates, activations, upstream, experts):
    width = activations.shape[1]
    shape = (experts, 2 * CAP, width)
    return pl.pallas_call(
        dispatch_kernel,
        out_shape=pltpu.HBM(shape, BF),
        in_specs=[HBM] * 4,
        out_specs=HBM,
        scratch_shapes=[
            pltpu.VMEM(routes.shape, jnp.int32), pltpu.VMEM(gates.shape, F32), pltpu.VMEM(activations.shape, BF),
            pltpu.VMEM(upstream.shape, BF), pltpu.VMEM(shape, BF), DMA((4,)), DMA((4,)),
        ],
        compiler_params=params(12),
        name="dispatch",
    )(*(in_hbm(array) for array in (routes, gates, activations, upstream)))


def tables_kernel(routes_ref, gates_ref, table_ref):
    slots = table_ref.shape[2]
    one, gate = slot_tables(routes_ref[...], gates_ref[...], slots // CAP)
    one, gate = one.T, gate.T
    high = gate.astype(BF)
    table_ref[0] = one.astype(BF)
    table_ref[1] = high
    table_ref[2] = (gate - high.astype(F32)).astype(BF)


def tables(routes, gates, experts):
    return pl.pallas_call(
        tables_kernel,
        out_shape=jax.ShapeDtypeStruct((3, routes.shape[1], experts * CAP), BF),
        in_specs=[VMEM] * 2,
        out_specs=VMEM,
        compiler_params=params(4),
        name="tables",
    )(routes, gates)


def combine_kernel(
    got_ref, table_hbm, mine_ref, theirs_ref, mixed_hbm, grad_hbm, wide_hbm, narrow_hbm, table_ref, wide_ref, narrow_ref,
    mixed_ref, grad_ref, in_sem, out_sem, wide_sem,
):
    load = pltpu.make_async_copy(table_hbm, table_ref, in_sem)
    load.start()
    total = mine_ref[...] + theirs_ref[...]
    tall, column = wide_ref.shape
    wide_ref[...] = total[:tall]
    for i in range(narrow_ref.shape[2] // column):
        for j in range(narrow_ref.shape[0]):
            at = tall + 8 * i + j
            narrow_ref[j, :, i * column : (i + 1) * column] = total[at : at + 1]
    stores = [
        pltpu.make_async_copy(wide_ref, wide_hbm, wide_sem.at[0]),
        pltpu.make_async_copy(narrow_ref, narrow_hbm, wide_sem.at[1]),
    ]
    for store in stores:
        store.start()
    experts = got_ref.shape[0]
    width = got_ref.shape[2]
    load.wait()
    one, high, low = table_ref[0], table_ref[1], table_ref[2]
    step = 512
    for i, lo in enumerate(range(0, width, step)):
        cols = slice(lo, lo + step)
        out = got_ref[:, :CAP, cols].reshape(experts * CAP, step)
        back = got_ref[:, CAP:, cols].reshape(experts * CAP, step)
        mixed_ref[:, cols] = (nn(high, out) + nn(low, out)).astype(BF)
        stores.append(pltpu.make_async_copy(mixed_ref.at[:, cols], mixed_hbm.at[:, cols], out_sem.at[0, i]))
        stores[-1].start()
        grad_ref[:, cols] = nn(one, back).astype(BF)
        stores.append(pltpu.make_async_copy(grad_ref.at[:, cols], grad_hbm.at[:, cols], out_sem.at[1, i]))
        stores[-1].start()
    for store in stores:
        store.wait()


def combine(got, table, mine, theirs, tall, inner):
    shape = (table.shape[1], got.shape[2])
    wide, narrow = (tall, mine.shape[1]), (3, 1, inner)
    return pl.pallas_call(
        combine_kernel,
        out_shape=(pltpu.HBM(shape, BF), pltpu.HBM(shape, BF), pltpu.HBM(wide, F32), pltpu.HBM(narrow, F32)),
        in_specs=[VMEM, HBM, VMEM, VMEM],
        out_specs=(HBM,) * 4,
        scratch_shapes=[
            pltpu.VMEM(table.shape, BF), pltpu.VMEM(wide, F32), pltpu.VMEM(narrow, F32), pltpu.VMEM(shape, BF),
            pltpu.VMEM(shape, BF), DMA, DMA((2, 4)), DMA((2,)),
        ],
        compiler_params=params(8),
        name="combine",
    )(in_vmem(got), in_hbm(table), mine, theirs)


def freeze_kernel(group_ref, *refs):
    levels, scales, adapters, frozen = refs[:3], refs[3:6], refs[6:12], refs[12:15]
    level_refs, scale_refs, adapter_refs = refs[15:18], refs[18:21], refs[21:27]
    in_sem, out_sem = refs[27:]

    @pl.when(group_ref[0] % 2 == FIRST_TO_FREEZE)
    def _():
        loads = [pltpu.make_async_copy(*pair, in_sem.at[i])
                 for i, pair in enumerate((*zip(scales, scale_refs), *zip(adapters, adapter_refs), *zip(levels, level_refs)))]
        for load in loads:
            load.start()
        for load in loads[:9]:
            load.wait()
        firsts = (adapter_refs[0], adapter_refs[1], adapter_refs[5])
        seconds = (adapter_refs[3], adapter_refs[4], adapter_refs[2])
        stores = []
        for i, (level_ref, scale_ref) in enumerate(zip(level_refs, scale_refs)):
            loads[9 + i].wait()
            for j in range(scale_ref.shape[0]):
                rows = slice(j * GROUP, (j + 1) * GROUP)
                scale = scale_ref[j] if len(scale_ref.shape) == 3 else scale_ref[j : j + 1, :]
                weight = (level_ref[rows, :].astype(F32) * scale).astype(BF)
                low = tn(firsts[i][:, rows], seconds[i][...])
                level_ref[rows, :] = (weight.astype(F32) + SCALING * low).astype(BF)
            stores.append(pltpu.make_async_copy(level_ref, frozen[i], out_sem.at[i]))
            stores[-1].start()
        for store in stores:
            store.wait()


def freeze(group, levels, scales, adapters):
    return pl.pallas_call(
        freeze_kernel,
        out_shape=tuple(pltpu.HBM(level.shape, BF) for level in levels),
        in_specs=[SMEM] + [HBM] * 12,
        out_specs=(HBM,) * 3,
        scratch_shapes=[
            *(pltpu.VMEM(level.shape, BF) for level in levels), *(pltpu.VMEM(scale.shape, F32) for scale in scales),
            *(pltpu.VMEM(adapter.shape, BF) for adapter in adapters), DMA((12,)), DMA((3,)),
        ],
        compiler_params=params(16),
        cost_estimate=cost(1 << 24, 1 << 24),
        name="freeze",
    )(group, *(in_hbm(array) for array in (*levels, *scales, *adapters)))


def expert_kernel(
    group_ref, got_ref, gate_hbm, up_hbm, down_hbm, gate_frozen_hbm, up_frozen_hbm, down_frozen_hbm,
    gate_scale_hbm, up_scale_hbm, down_scale_hbm, gate_first_hbm, up_first_hbm, down_second_hbm,
    gate_second_hbm, up_second_hbm, down_first_hbm, send_hbm, keep_hbm, other_hbm,
    gate_ref, up_ref, down_ref, gate_scale_ref, up_scale_ref, down_scale_ref, wide_ref, narrow_ref, send_ref,
    inside_ref, down_low_ref, back_both_ref, piece_ref, rounded_ref, level_sem, small_sem, scale_sem, out_sem, piece_sem,
):
    experts, _, width = got_ref.shape
    rows = experts * CAP
    inner = gate_ref.shape[1]
    rank = gate_first_hbm.shape[0]
    step = 256

    pairs = [(source, wide_ref.at[i * rank : (i + 1) * rank, :])
             for i, source in enumerate((gate_first_hbm, up_first_hbm, down_second_hbm))]
    pairs += [(down_second_hbm, down_ref.at[inner : inner + rank, :])]
    pairs += [(source, narrow_ref.at[i * rank : (i + 1) * rank, :])
              for i, source in enumerate((gate_second_hbm, up_second_hbm, down_first_hbm))]
    small = [pltpu.make_async_copy(source, target, small_sem.at[i]) for i, (source, target) in enumerate(pairs)]
    for copy in small:
        copy.start()
    ready = group_ref[0] % 2 == FIRST_TO_FREEZE
    raw = ((gate_hbm, gate_ref), (up_hbm, up_ref), (down_hbm, down_ref))
    frozen = ((gate_frozen_hbm, gate_ref), (up_frozen_hbm, up_ref), (down_frozen_hbm, down_ref))
    pieces = [(part, kind) for part in range(inner // step) for kind in range(3)]

    def loads(weights, some):
        copies = []
        for part, kind in some:
            cols = slice(part * step, (part + 1) * step)
            place = (cols, slice(0, width)) if kind == 2 else (slice(0, width), cols)
            source, target = weights[kind]
            copies.append(pltpu.make_async_copy(source.at[place], target.at[place], level_sem.at[part, kind]))
        return copies

    scales = (gate_scale_ref, up_scale_ref, down_scale_ref)
    scale_loads = [pltpu.make_async_copy(source, target, scale_sem.at[i]) for i, (source, target) in enumerate(
        zip((gate_scale_hbm, up_scale_hbm, down_scale_hbm), scales))]

    @pl.when(jnp.logical_not(ready))
    def _():
        for copy in scale_loads:
            copy.start()

    def start(some):
        for condition, weights in ((ready, frozen), (jnp.logical_not(ready), raw)):

            @pl.when(condition)
            def _(weights=weights):
                for copy in loads(weights, some):
                    copy.start()

    start(pieces[:2])
    down_ref[inner + rank :, :] = jnp.zeros((GROUP - rank, width), BF)

    def land(part, kinds, folded):
        for copy in loads(raw, [(part, kind) for kind in kinds]):
            copy.wait()
        if folded:
            return
        cols = slice(part * step, (part + 1) * step)
        for target, scale_ref in ((gate_ref, gate_scale_ref), (up_ref, up_scale_ref)) if 0 in kinds else ():
            for i in range(width // GROUP):
                group = slice(i * GROUP, (i + 1) * GROUP)
                target[group, cols] = (target[group, cols].astype(F32) * scale_ref[i : i + 1, cols]).astype(BF)
        for i in range(part * step // GROUP, (part + 1) * step // GROUP) if 2 in kinds else ():
            group = slice(i * GROUP, (i + 1) * GROUP)
            down_ref[group, :] = (down_ref[group, :].astype(F32) * down_scale_ref[i]).astype(BF)

    x = got_ref[:, :CAP, :].reshape(rows, width)
    g = got_ref[:, CAP:, :].reshape(rows, width)
    first_ref = wide_ref.at[: 2 * rank, :]
    down_second_ref = wide_ref.at[2 * rank :, :]
    gate_second_ref = narrow_ref.at[:rank, :]
    up_second_ref = narrow_ref.at[rank : 2 * rank, :]
    down_first_ref = narrow_ref.at[2 * rank :, :]
    for copy in small:
        copy.wait()
    start(pieces[2:])

    @pl.when(jnp.logical_not(ready))
    def _():
        for copy in scale_loads:
            copy.wait()

    first_low = nt(x, first_ref[...]).astype(BF)
    gate_low, up_low = first_low[:, :rank], first_low[:, rank:]
    back_down = nt(g, down_second_ref[...]).astype(BF)
    half = jnp.asarray(SCALING, BF)
    sends = {}
    for index, hi in enumerate(SPLITS):
        cols = slice(hi - SPLITS[hi], hi)
        sends[hi] = pltpu.make_async_copy(send_ref.at[:, :, cols], send_hbm.at[:, :, cols], out_sem.at[index])

    def both_ways(folded):
        down_low = jnp.zeros((rows, rank), F32)
        back_gate = jnp.zeros((rows, rank), F32)
        back_up = jnp.zeros((rows, rank), F32)
        for part, kind in pieces:
            if kind == 0:
                land(part, (0, 1) if part in SPLIT else (0, 1, 2), folded)
            if kind == 2 and part in SPLIT:
                land(part, (2,), folded)
            cols = slice(part * step, (part + 1) * step)
            if kind == 0:
                gate_pre = nn(x, gate_ref[:, cols])
                if not folded:
                    gate_pre = gate_pre + nn(gate_low * half, gate_second_ref[:, cols])
                logistic = jax.nn.sigmoid(gate_pre)
                activated = gate_pre * logistic
                slope = logistic * (1.0 + gate_pre * (1.0 - logistic))
            elif kind == 1:
                up_pre = nn(x, up_ref[:, cols])
                if not folded:
                    up_pre = up_pre + nn(up_low * half, up_second_ref[:, cols])
                hidden = (activated * up_pre).astype(BF)
                inside_ref[0, :, cols] = hidden
                down_low += nt(hidden, down_first_ref[:, cols])
            else:
                d_hidden = nt(g, down_ref[cols, :])
                if not folded:
                    d_hidden = d_hidden + nn(back_down * half, down_first_ref[:, cols])
                d_gate = (d_hidden * up_pre * slope).astype(BF)
                d_up = (d_hidden * activated).astype(BF)
                inside_ref[1, :, cols] = d_gate
                inside_ref[2, :, cols] = d_up
                back_gate += nt(d_gate, gate_second_ref[:, cols])
                back_up += nt(d_up, up_second_ref[:, cols])
        down_low = down_low.astype(BF)
        back_both = jnp.concatenate([back_gate, back_up], axis=1).astype(BF)
        down_low_ref[...] = down_low
        back_both_ref[...] = back_both
        hidden, d_gate, d_up = inside_ref[0], inside_ref[1], inside_ref[2]
        if not folded:
            hidden = jnp.concatenate([hidden, down_low * half, jnp.zeros((rows, GROUP - rank), BF)], axis=1)
        for lo in range(0, width, step):
            cols = slice(lo, lo + step)
            out = nn(hidden, down_ref[: hidden.shape[1], cols])
            send_ref[:, :CAP, cols] = out.astype(BF).reshape(experts, CAP, step)
            back = nt(d_gate, gate_ref[cols, :]) + nt(d_up, up_ref[cols, :])
            if not folded:
                back = back + nn(back_both * half, first_ref[:, cols])
            send_ref[:, CAP:, cols] = back.astype(BF).reshape(experts, CAP, step)
            if lo + step in SPLITS:
                sends[lo + step].start()

    @pl.when(ready)
    def _():
        both_ways(True)

    @pl.when(jnp.logical_not(ready))
    def _():
        both_ways(False)

    stores = list(sends.values())
    hidden, d_gate, d_up = inside_ref[0], inside_ref[1], inside_ref[2]
    down_low, back_both = down_low_ref[...], back_both_ref[...]
    groups = piece_ref.shape[0]
    column = width // groups
    for lo in range(0, width, 512):
        cols = slice(lo, lo + 512)
        both = SCALING * tn(back_both, got_ref[:, :CAP, cols].reshape(rows, 512))
        down = SCALING * tn(down_low, got_ref[:, CAP:, cols].reshape(rows, 512))
        for i in range(512 // column):
            part = slice(i * column, (i + 1) * column)
            piece_ref[lo // column + i, : 2 * rank, :] = both[:, part]
            piece_ref[lo // column + i, 2 * rank : 3 * rank, :] = down[:, part]
    source = lax.broadcasted_iota(jnp.int32, (rank, 8 * rank), 0)
    target = lax.broadcasted_iota(jnp.int32, (rank, 8 * rank), 1)
    narrow = jnp.zeros((8 * rank, inner), F32)
    for i, (left, right) in enumerate(((gate_low, d_gate), (up_low, d_up), (back_down, hidden))):
        spread = jnp.where(target == 8 * source + i, SCALING, 0.0).astype(BF)
        narrow += tn(nn(left, spread).astype(BF), right)
    for piece in range(groups):
        for i in range(inner // column):
            at = 3 * rank + 8 * i
            piece_ref[piece, at : at + 8, :] = narrow[8 * piece : 8 * piece + 8, i * column : (i + 1) * column]
    group = group_ref[0]
    side = group % 2
    plane = group // 2
    rounded_ref[...] = piece_ref[...].astype(BF)
    half = groups // 4
    for place in range(groups // 2):
        turned = (place & 1) * 4 + (place & 2) + (place >> 2)
        other = lax.bitwise_xor(plane, jnp.int32(turned))
        source, target = (piece_ref, keep_hbm) if place < half else (rounded_ref, other_hbm)
        for i, core in enumerate((side, 1 - side)):
            copy = pltpu.make_async_copy(
                source.at[2 * other + core], target.at[place % half, i], piece_sem.at[place, i]
            )
            stores.append(copy)
            copy.start()
    for store in stores:
        store.wait()


def expert(group, groups, got, levels, frozen, scales, wide, narrow):
    rows = got.shape[0] * CAP
    width = got.shape[2]
    inner = levels[0].shape[1]
    rank = wide[0].shape[0]
    column = width // groups
    height = 3 * rank + 8 * (inner // column)
    part = (groups // 4, 2, height, column)
    return pl.pallas_call(
        expert_kernel,
        out_shape=(pltpu.HBM(got.shape, BF), pltpu.HBM(part, F32), pltpu.HBM(part, BF)),
        in_specs=[SMEM, VMEM] + [HBM] * 15,
        out_specs=(HBM,) * 3,
        scratch_shapes=[
            pltpu.VMEM(levels[0].shape, BF), pltpu.VMEM(levels[1].shape, BF), pltpu.VMEM((inner + GROUP, width), BF),
            *(pltpu.VMEM(scale.shape, F32) for scale in scales),
            pltpu.VMEM((3 * rank, width), BF), pltpu.VMEM((3 * rank, inner), BF),
            pltpu.VMEM(got.shape, BF), pltpu.VMEM((3, rows, inner), BF), pltpu.VMEM((rows, rank), BF),
            pltpu.VMEM((rows, 2 * rank), BF), pltpu.VMEM((groups, height, column), F32),
            pltpu.VMEM((groups, height, column), BF),
            DMA((inner // 256, 3)), DMA((7,)), DMA((3,)), DMA((width // 256,)), DMA((groups // 2, 2)),
        ],
        compiler_params=params(32),
        name="expert",
    )(group, in_vmem(got), *(in_hbm(array) for array in (*levels, *frozen, *scales, *wide, *narrow)))


def shards(
    activations, routes, gates, gate_levels, gate_scales, up_levels, up_scales, down_levels, down_scales,
    gate_adapter_first, gate_adapter_second, up_adapter_first, up_adapter_second,
    down_adapter_first, down_adapter_second, upstream,
):
    experts = lax.axis_size("expert")
    groups = lax.axis_size("dp")
    width = activations.shape[1]
    inner = gate_levels.shape[2]
    rank = gate_adapter_first.shape[1]

    routes, gates = routes.T, gates.T
    group = lax.axis_index("dp").astype(jnp.int32).reshape(1)
    levels = (gate_levels[0], up_levels[0], down_levels[0])
    scales = (gate_scales[0], up_scales[0], down_scales.transpose(1, 0, 2))
    wide = (gate_adapter_first[0], up_adapter_first[0], down_adapter_second[0])
    narrow = (gate_adapter_second[0], up_adapter_second[0], down_adapter_first[0])
    frozen = freeze(group, levels, scales, wide + narrow)
    routes, gates, frozen = lax.optimization_barrier((routes, gates, frozen))
    send = dispatch(routes, gates, activations, upstream, experts)
    send, group, frozen = lax.optimization_barrier((send, group, frozen))
    got = lax.all_to_all(send, "expert", split_axis=0, concat_axis=0, tiled=True)

    send, keep, other = expert(
        group,
        groups,
        got,
        levels,
        frozen,
        scales,
        wide,
        narrow,
    )
    routes, gates, keep = lax.optimization_barrier((routes, gates, keep))
    table = tables(routes, gates, experts)
    back = lax.all_to_all(send, "expert", split_axis=0, concat_axis=0, tiled=True)

    def swap(part, mask):
        return lax.ppermute(part, "dp", [(i, i ^ mask) for i in range(groups)])

    total = keep + swap(other, 2).astype(F32)
    sent = total.astype(BF)
    total = total[0] + (swap(sent[1], 8).astype(F32) + swap(sent[2], 4).astype(F32) + swap(sent[3], 12).astype(F32))
    mixed, input_grad, grad_wide, grad_narrow = combine(back, table, total[0], swap(total[1], 1), 3 * rank, inner)
    grad_wide = grad_wide.reshape(1, 3, rank, width // groups)
    grad_narrow = grad_narrow.reshape(1, 3, 1, inner)
    return mixed, input_grad, grad_wide, grad_narrow


def solution(mesh):
    rows = P(("dp", "expert"), None)
    weight = P("expert", None, None)
    return jax.shard_map(
        shards,
        mesh=mesh,
        in_specs=(rows,) * 3 + (weight,) * 12 + (rows,),
        out_specs=(rows, rows, P("expert", None, None, "dp"), P("expert", None, "dp", None)),
        check_vma=False,
    )
```

```python
import jax
import jax.numpy as jnp
from jax import lax
from jax.experimental import pallas as pl
from jax.experimental.pallas import tpu as pltpu
from jax.sharding import PartitionSpec as P

GROUP = 128
FIRST_TO_FREEZE = 0
SPLIT = (0,)
CAP = 16
SCALING = 0.5
BF = jnp.bfloat16
F32 = jnp.float32
VMEM = pl.BlockSpec(memory_space=pltpu.VMEM)
SMEM = pl.BlockSpec(memory_space=pltpu.SMEM)
HBM = pl.BlockSpec(memory_space=pltpu.HBM)
DMA = pltpu.SemaphoreType.DMA
SPLITS = {1536: 1536, 2048: 512}


def nn(a, b):
    return lax.dot_general(a, b, (((1,), (0,)), ((), ())), preferred_element_type=F32)


def nt(a, b):
    return lax.dot_general(a, b, (((1,), (1,)), ((), ())), preferred_element_type=F32)


def tn(a, b):
    return lax.dot_general(a, b, (((0,), (0,)), ((), ())), preferred_element_type=F32)


def params(mebibytes):
    return pltpu.CompilerParams(vmem_limit_bytes=mebibytes * 1024 * 1024)


def cost(flops, bytes_accessed):
    return pl.CostEstimate(flops=flops, bytes_accessed=bytes_accessed, transcendentals=0)


def in_vmem(array):
    return pltpu.with_memory_space_constraint(array, pltpu.VMEM)


def in_hbm(array):
    return pltpu.with_memory_space_constraint(array, pltpu.HBM)


def slot_tables(routes, gates_t, experts):
    top, tokens = routes.shape
    routes_t = routes.astype(F32)
    column = lax.broadcasted_iota(jnp.int32, (experts, tokens), 0).astype(F32)
    named = jnp.zeros((experts, tokens), F32)
    weight = jnp.zeros((experts, tokens), F32)
    for k in range(top):
        hit = routes_t[k : k + 1, :] == column
        named = named + jnp.where(hit, 1.0, 0.0)
        weight = weight + jnp.where(hit, gates_t[k : k + 1, :], 0.0)
    earlier = lax.broadcasted_iota(jnp.int32, (tokens, tokens), 0)
    later = lax.broadcasted_iota(jnp.int32, (tokens, tokens), 1)
    before = jnp.where(earlier < later, 1.0, 0.0).astype(BF)
    place = nn(named.astype(BF), before)
    place = jnp.where(named > 0.0, place, -1.0)
    slot = lax.broadcasted_iota(jnp.int32, (experts, CAP, tokens), 1).astype(F32)
    taken = place[:, None, :] == slot
    one = jnp.where(taken, 1.0, 0.0).reshape(experts * CAP, tokens)
    gate = jnp.where(taken, weight[:, None, :], 0.0).reshape(experts * CAP, tokens)
    return one, gate


def dispatch_kernel(
    routes_hbm, gates_hbm, act_hbm, up_hbm, send_hbm, routes_ref, gates_ref, act_ref, up_ref, send_ref, in_sem, out_sem
):
    experts = send_ref.shape[0]
    width = act_ref.shape[1]
    pairs = ((routes_hbm, routes_ref), (gates_hbm, gates_ref), (act_hbm, act_ref), (up_hbm, up_ref))
    loads = [pltpu.make_async_copy(source, target, in_sem.at[i]) for i, (source, target) in enumerate(pairs)]
    for load in loads:
        load.start()
    loads[0].wait()
    loads[1].wait()
    one, gate = slot_tables(routes_ref[...], gates_ref[...], experts)
    one = one.astype(BF)
    weight = jnp.sum(gate, axis=1, keepdims=True)
    loads[2].wait()
    loads[3].wait()
    step = 512
    stores = []
    for i, lo in enumerate(range(0, width, step)):
        cols = slice(lo, lo + step)
        send_ref[:, :CAP, cols] = nn(one, act_ref[:, cols]).astype(BF).reshape(experts, CAP, step)
        picked = weight * nn(one, up_ref[:, cols])
        send_ref[:, CAP:, cols] = picked.astype(BF).reshape(experts, CAP, step)
        store = pltpu.make_async_copy(send_ref.at[:, :, cols], send_hbm.at[:, :, cols], out_sem.at[i])
        store.start()
        stores.append(store)
    for store in stores:
        store.wait()


def dispatch(routes, gates, activations, upstream, experts):
    width = activations.shape[1]
    shape = (experts, 2 * CAP, width)
    return pl.pallas_call(
        dispatch_kernel,
        out_shape=pltpu.HBM(shape, BF),
        in_specs=[HBM] * 4,
        out_specs=HBM,
        scratch_shapes=[
            pltpu.VMEM(routes.shape, jnp.int32), pltpu.VMEM(gates.shape, F32), pltpu.VMEM(activations.shape, BF),
            pltpu.VMEM(upstream.shape, BF), pltpu.VMEM(shape, BF), DMA((4,)), DMA((4,)),
        ],
        compiler_params=params(12),
        name="dispatch",
    )(*(in_hbm(array) for array in (routes, gates, activations, upstream)))


def tables_kernel(routes_ref, gates_ref, table_ref):
    slots = table_ref.shape[2]
    one, gate = slot_tables(routes_ref[...], gates_ref[...], slots // CAP)
    one, gate = one.T, gate.T
    high = gate.astype(BF)
    table_ref[0] = one.astype(BF)
    table_ref[1] = high
    table_ref[2] = (gate - high.astype(F32)).astype(BF)


def tables(routes, gates, experts):
    return pl.pallas_call(
        tables_kernel,
        out_shape=jax.ShapeDtypeStruct((3, routes.shape[1], experts * CAP), BF),
        in_specs=[VMEM] * 2,
        out_specs=VMEM,
        compiler_params=params(4),
        name="tables",
    )(routes, gates)


def combine_kernel(
    got_ref, table_hbm, mine_ref, theirs_ref, mixed_hbm, grad_hbm, wide_hbm, narrow_hbm, table_ref, wide_ref, narrow_ref,
    mixed_ref, grad_ref, in_sem, out_sem, wide_sem,
):
    load = pltpu.make_async_copy(table_hbm, table_ref, in_sem)
    load.start()
    total = mine_ref[...] + theirs_ref[...]
    tall, column = wide_ref.shape
    wide_ref[...] = total[:tall]
    for i in range(narrow_ref.shape[2] // column):
        for j in range(narrow_ref.shape[0]):
            at = tall + 8 * i + j
            narrow_ref[j, :, i * column : (i + 1) * column] = total[at : at + 1]
    stores = [
        pltpu.make_async_copy(wide_ref, wide_hbm, wide_sem.at[0]),
        pltpu.make_async_copy(narrow_ref, narrow_hbm, wide_sem.at[1]),
    ]
    for store in stores:
        store.start()
    experts = got_ref.shape[0]
    width = got_ref.shape[2]
    load.wait()
    one, high, low = table_ref[0], table_ref[1], table_ref[2]
    step = 512
    for i, lo in enumerate(range(0, width, step)):
        cols = slice(lo, lo + step)
        out = got_ref[:, :CAP, cols].reshape(experts * CAP, step)
        back = got_ref[:, CAP:, cols].reshape(experts * CAP, step)
        mixed_ref[:, cols] = (nn(high, out) + nn(low, out)).astype(BF)
        stores.append(pltpu.make_async_copy(mixed_ref.at[:, cols], mixed_hbm.at[:, cols], out_sem.at[0, i]))
        stores[-1].start()
        grad_ref[:, cols] = nn(one, back).astype(BF)
        stores.append(pltpu.make_async_copy(grad_ref.at[:, cols], grad_hbm.at[:, cols], out_sem.at[1, i]))
        stores[-1].start()
    for store in stores:
        store.wait()


def combine(got, table, mine, theirs, tall, inner):
    shape = (table.shape[1], got.shape[2])
    wide, narrow = (tall, mine.shape[1]), (3, 1, inner)
    return pl.pallas_call(
        combine_kernel,
        out_shape=(pltpu.HBM(shape, BF), pltpu.HBM(shape, BF), pltpu.HBM(wide, F32), pltpu.HBM(narrow, F32)),
        in_specs=[VMEM, HBM, VMEM, VMEM],
        out_specs=(HBM,) * 4,
        scratch_shapes=[
            pltpu.VMEM(table.shape, BF), pltpu.VMEM(wide, F32), pltpu.VMEM(narrow, F32), pltpu.VMEM(shape, BF),
            pltpu.VMEM(shape, BF), DMA, DMA((2, 4)), DMA((2,)),
        ],
        compiler_params=params(8),
        name="combine",
    )(in_vmem(got), in_hbm(table), mine, theirs)


def freeze_kernel(group_ref, *refs):
    levels, scales, adapters, frozen = refs[:3], refs[3:6], refs[6:12], refs[12:15]
    level_refs, scale_refs, adapter_refs = refs[15:18], refs[18:21], refs[21:27]
    in_sem, out_sem = refs[27:]

    @pl.when(group_ref[0] % 2 == FIRST_TO_FREEZE)
    def _():
        loads = [pltpu.make_async_copy(*pair, in_sem.at[i])
                 for i, pair in enumerate((*zip(scales, scale_refs), *zip(adapters, adapter_refs), *zip(levels, level_refs)))]
        for load in loads:
            load.start()
        for load in loads[:9]:
            load.wait()
        firsts = (adapter_refs[0], adapter_refs[1], adapter_refs[5])
        seconds = (adapter_refs[3], adapter_refs[4], adapter_refs[2])
        stores = []
        for i, (level_ref, scale_ref) in enumerate(zip(level_refs, scale_refs)):
            loads[9 + i].wait()
            for j in range(scale_ref.shape[0]):
                rows = slice(j * GROUP, (j + 1) * GROUP)
                scale = scale_ref[j] if len(scale_ref.shape) == 3 else scale_ref[j : j + 1, :]
                weight = (level_ref[rows, :].astype(F32) * scale).astype(BF)
                low = tn(firsts[i][:, rows], seconds[i][...])
                level_ref[rows, :] = (weight.astype(F32) + SCALING * low).astype(BF)
            stores.append(pltpu.make_async_copy(level_ref, frozen[i], out_sem.at[i]))
            stores[-1].start()
        for store in stores:
            store.wait()


def freeze(group, levels, scales, adapters):
    return pl.pallas_call(
        freeze_kernel,
        out_shape=tuple(pltpu.HBM(level.shape, BF) for level in levels),
        in_specs=[SMEM] + [HBM] * 12,
        out_specs=(HBM,) * 3,
        scratch_shapes=[
            *(pltpu.VMEM(level.shape, BF) for level in levels), *(pltpu.VMEM(scale.shape, F32) for scale in scales),
            *(pltpu.VMEM(adapter.shape, BF) for adapter in adapters), DMA((12,)), DMA((3,)),
        ],
        compiler_params=params(16),
        cost_estimate=cost(1 << 24, 1 << 24),
        name="freeze",
    )(group, *(in_hbm(array) for array in (*levels, *scales, *adapters)))


def expert_kernel(
    group_ref, got_ref, gate_hbm, up_hbm, down_hbm, gate_frozen_hbm, up_frozen_hbm, down_frozen_hbm,
    gate_scale_hbm, up_scale_hbm, down_scale_hbm, gate_first_hbm, up_first_hbm, down_second_hbm,
    gate_second_hbm, up_second_hbm, down_first_hbm, send_hbm, keep_hbm, other_hbm,
    gate_ref, up_ref, down_ref, gate_scale_ref, up_scale_ref, down_scale_ref, wide_ref, narrow_ref, send_ref,
    inside_ref, down_low_ref, back_both_ref, piece_ref, keep_ref, other_ref, level_sem, small_sem, scale_sem, out_sem, piece_sem,
):
    experts, _, width = got_ref.shape
    rows = experts * CAP
    inner = gate_ref.shape[1]
    rank = gate_first_hbm.shape[0]
    step = 256

    pairs = [(source, wide_ref.at[i * rank : (i + 1) * rank, :])
             for i, source in enumerate((gate_first_hbm, up_first_hbm, down_second_hbm))]
    pairs += [(down_second_hbm, down_ref.at[inner : inner + rank, :])]
    pairs += [(source, narrow_ref.at[i * rank : (i + 1) * rank, :])
              for i, source in enumerate((gate_second_hbm, up_second_hbm, down_first_hbm))]
    small = [pltpu.make_async_copy(source, target, small_sem.at[i]) for i, (source, target) in enumerate(pairs)]
    for copy in small:
        copy.start()
    ready = group_ref[0] % 2 == FIRST_TO_FREEZE
    raw = ((gate_hbm, gate_ref), (up_hbm, up_ref), (down_hbm, down_ref))
    frozen = ((gate_frozen_hbm, gate_ref), (up_frozen_hbm, up_ref), (down_frozen_hbm, down_ref))
    pieces = [(part, kind) for part in range(inner // step) for kind in range(3)]

    def loads(weights, some):
        copies = []
        for part, kind in some:
            cols = slice(part * step, (part + 1) * step)
            place = (cols, slice(0, width)) if kind == 2 else (slice(0, width), cols)
            source, target = weights[kind]
            copies.append(pltpu.make_async_copy(source.at[place], target.at[place], level_sem.at[part, kind]))
        return copies

    scales = (gate_scale_ref, up_scale_ref, down_scale_ref)
    scale_loads = [pltpu.make_async_copy(source, target, scale_sem.at[i]) for i, (source, target) in enumerate(
        zip((gate_scale_hbm, up_scale_hbm, down_scale_hbm), scales))]

    @pl.when(jnp.logical_not(ready))
    def _():
        for copy in scale_loads:
            copy.start()

    def start(some):
        for condition, weights in ((ready, frozen), (jnp.logical_not(ready), raw)):

            @pl.when(condition)
            def _(weights=weights):
                for copy in loads(weights, some):
                    copy.start()

    start(pieces[:2])
    down_ref[inner + rank :, :] = jnp.zeros((GROUP - rank, width), BF)

    def land(part, kinds, folded):
        for copy in loads(raw, [(part, kind) for kind in kinds]):
            copy.wait()
        if folded:
            return
        cols = slice(part * step, (part + 1) * step)
        for target, scale_ref in ((gate_ref, gate_scale_ref), (up_ref, up_scale_ref)) if 0 in kinds else ():
            for i in range(width // GROUP):
                group = slice(i * GROUP, (i + 1) * GROUP)
                target[group, cols] = (target[group, cols].astype(F32) * scale_ref[i : i + 1, cols]).astype(BF)
        for i in range(part * step // GROUP, (part + 1) * step // GROUP) if 2 in kinds else ():
            group = slice(i * GROUP, (i + 1) * GROUP)
            down_ref[group, :] = (down_ref[group, :].astype(F32) * down_scale_ref[i]).astype(BF)

    x = got_ref[:, :CAP, :].reshape(rows, width)
    g = got_ref[:, CAP:, :].reshape(rows, width)
    first_ref = wide_ref.at[: 2 * rank, :]
    down_second_ref = wide_ref.at[2 * rank :, :]
    gate_second_ref = narrow_ref.at[:rank, :]
    up_second_ref = narrow_ref.at[rank : 2 * rank, :]
    down_first_ref = narrow_ref.at[2 * rank :, :]
    for copy in small:
        copy.wait()
    start(pieces[2:])

    @pl.when(jnp.logical_not(ready))
    def _():
        for copy in scale_loads:
            copy.wait()

    first_low = nt(x, first_ref[...]).astype(BF)
    gate_low, up_low = first_low[:, :rank], first_low[:, rank:]
    back_down = nt(g, down_second_ref[...]).astype(BF)
    half = jnp.asarray(SCALING, BF)
    sends = {}
    for index, hi in enumerate(SPLITS):
        cols = slice(hi - SPLITS[hi], hi)
        sends[hi] = pltpu.make_async_copy(send_ref.at[:, :, cols], send_hbm.at[:, :, cols], out_sem.at[index])

    def both_ways(folded):
        down_low = jnp.zeros((rows, rank), F32)
        back_gate = jnp.zeros((rows, rank), F32)
        back_up = jnp.zeros((rows, rank), F32)
        for part, kind in pieces:
            if kind == 0:
                land(part, (0, 1) if part in SPLIT else (0, 1, 2), folded)
            if kind == 2 and part in SPLIT:
                land(part, (2,), folded)
            cols = slice(part * step, (part + 1) * step)
            if kind == 0:
                gate_pre = nn(x, gate_ref[:, cols])
                if not folded:
                    gate_pre = gate_pre + nn(gate_low * half, gate_second_ref[:, cols])
                logistic = jax.nn.sigmoid(gate_pre)
                activated = gate_pre * logistic
                slope = logistic * (1.0 + gate_pre * (1.0 - logistic))
            elif kind == 1:
                up_pre = nn(x, up_ref[:, cols])
                if not folded:
                    up_pre = up_pre + nn(up_low * half, up_second_ref[:, cols])
                hidden = (activated * up_pre).astype(BF)
                inside_ref[0, :, cols] = hidden
                down_low += nt(hidden, down_first_ref[:, cols])
            else:
                d_hidden = nt(g, down_ref[cols, :])
                if not folded:
                    d_hidden = d_hidden + nn(back_down * half, down_first_ref[:, cols])
                d_gate = (d_hidden * up_pre * slope).astype(BF)
                d_up = (d_hidden * activated).astype(BF)
                inside_ref[1, :, cols] = d_gate
                inside_ref[2, :, cols] = d_up
                back_gate += nt(d_gate, gate_second_ref[:, cols])
                back_up += nt(d_up, up_second_ref[:, cols])
        down_low = down_low.astype(BF)
        back_both = jnp.concatenate([back_gate, back_up], axis=1).astype(BF)
        down_low_ref[...] = down_low
        back_both_ref[...] = back_both
        hidden, d_gate, d_up = inside_ref[0], inside_ref[1], inside_ref[2]
        if not folded:
            hidden = jnp.concatenate([hidden, down_low * half, jnp.zeros((rows, GROUP - rank), BF)], axis=1)
        for lo in range(0, width, step):
            cols = slice(lo, lo + step)
            out = nn(hidden, down_ref[: hidden.shape[1], cols])
            send_ref[:, :CAP, cols] = out.astype(BF).reshape(experts, CAP, step)
            back = nt(d_gate, gate_ref[cols, :]) + nt(d_up, up_ref[cols, :])
            if not folded:
                back = back + nn(back_both * half, first_ref[:, cols])
            send_ref[:, CAP:, cols] = back.astype(BF).reshape(experts, CAP, step)
            if lo + step in SPLITS:
                sends[lo + step].start()

    @pl.when(ready)
    def _():
        both_ways(True)

    @pl.when(jnp.logical_not(ready))
    def _():
        both_ways(False)

    stores = list(sends.values())
    hidden, d_gate, d_up = inside_ref[0], inside_ref[1], inside_ref[2]
    down_low, back_both = down_low_ref[...], back_both_ref[...]
    groups = piece_ref.shape[0]
    column = width // groups
    for lo in range(0, width, 512):
        cols = slice(lo, lo + 512)
        both = SCALING * tn(back_both, got_ref[:, :CAP, cols].reshape(rows, 512))
        down = SCALING * tn(down_low, got_ref[:, CAP:, cols].reshape(rows, 512))
        for i in range(512 // column):
            part = slice(i * column, (i + 1) * column)
            piece_ref[lo // column + i, : 2 * rank, :] = both[:, part]
            piece_ref[lo // column + i, 2 * rank : 3 * rank, :] = down[:, part]
    source = lax.broadcasted_iota(jnp.int32, (rank, 8 * rank), 0)
    target = lax.broadcasted_iota(jnp.int32, (rank, 8 * rank), 1)
    narrow = jnp.zeros((8 * rank, inner), F32)
    for i, (left, right) in enumerate(((gate_low, d_gate), (up_low, d_up), (back_down, hidden))):
        spread = jnp.where(target == 8 * source + i, SCALING, 0.0).astype(BF)
        narrow += tn(nn(left, spread).astype(BF), right)
    for piece in range(groups):
        for i in range(inner // column):
            at = 3 * rank + 8 * i
            piece_ref[piece, at : at + 8, :] = narrow[8 * piece : 8 * piece + 8, i * column : (i + 1) * column]
    group = group_ref[0]
    side = group % 2
    plane = group // 2
    half = groups // 4
    for place in range(groups // 2):
        turned = (place & 1) * 4 + (place & 2) + (place >> 2)
        other = lax.bitwise_xor(plane, jnp.int32(turned))
        for i, core in enumerate((side, 1 - side)):
            piece = piece_ref[2 * other + core]
            if place < half:
                keep_ref[place, i] = piece
            else:
                other_ref[place - half, i] = piece.astype(BF)
    stores += [
        pltpu.make_async_copy(keep_ref, keep_hbm, piece_sem.at[0]),
        pltpu.make_async_copy(other_ref, other_hbm, piece_sem.at[1]),
    ]
    for store in stores[-2:]:
        store.start()
    for store in stores:
        store.wait()


def expert(group, groups, got, levels, frozen, scales, wide, narrow):
    rows = got.shape[0] * CAP
    width = got.shape[2]
    inner = levels[0].shape[1]
    rank = wide[0].shape[0]
    column = width // groups
    height = 3 * rank + 8 * (inner // column)
    part = (groups // 4, 2, height, column)
    return pl.pallas_call(
        expert_kernel,
        out_shape=(pltpu.HBM(got.shape, BF), pltpu.HBM(part, F32), pltpu.HBM(part, BF)),
        in_specs=[SMEM, VMEM] + [HBM] * 15,
        out_specs=(HBM,) * 3,
        scratch_shapes=[
            pltpu.VMEM(levels[0].shape, BF), pltpu.VMEM(levels[1].shape, BF), pltpu.VMEM((inner + GROUP, width), BF),
            *(pltpu.VMEM(scale.shape, F32) for scale in scales),
            pltpu.VMEM((3 * rank, width), BF), pltpu.VMEM((3 * rank, inner), BF),
            pltpu.VMEM(got.shape, BF), pltpu.VMEM((3, rows, inner), BF), pltpu.VMEM((rows, rank), BF),
            pltpu.VMEM((rows, 2 * rank), BF), pltpu.VMEM((groups, height, column), F32),
            pltpu.VMEM(part, F32), pltpu.VMEM(part, BF),
            DMA((inner // 256, 3)), DMA((7,)), DMA((3,)), DMA((width // 256,)), DMA((2,)),
        ],
        compiler_params=params(32),
        name="expert",
    )(group, in_vmem(got), *(in_hbm(array) for array in (*levels, *frozen, *scales, *wide, *narrow)))


def shards(
    activations, routes, gates, gate_levels, gate_scales, up_levels, up_scales, down_levels, down_scales,
    gate_adapter_first, gate_adapter_second, up_adapter_first, up_adapter_second,
    down_adapter_first, down_adapter_second, upstream,
):
    experts = lax.axis_size("expert")
    groups = lax.axis_size("dp")
    width = activations.shape[1]
    inner = gate_levels.shape[2]
    rank = gate_adapter_first.shape[1]

    routes, gates = routes.T, gates.T
    group = lax.axis_index("dp").astype(jnp.int32).reshape(1)
    levels = (gate_levels[0], up_levels[0], down_levels[0])
    scales = (gate_scales[0], up_scales[0], down_scales.transpose(1, 0, 2))
    wide = (gate_adapter_first[0], up_adapter_first[0], down_adapter_second[0])
    narrow = (gate_adapter_second[0], up_adapter_second[0], down_adapter_first[0])
    frozen = freeze(group, levels, scales, wide + narrow)
    routes, gates, frozen = lax.optimization_barrier((routes, gates, frozen))
    send = dispatch(routes, gates, activations, upstream, experts)
    send, group, frozen = lax.optimization_barrier((send, group, frozen))
    got = lax.all_to_all(send, "expert", split_axis=0, concat_axis=0, tiled=True)

    send, keep, other = expert(
        group,
        groups,
        got,
        levels,
        frozen,
        scales,
        wide,
        narrow,
    )
    routes, gates, keep = lax.optimization_barrier((routes, gates, keep))
    table = tables(routes, gates, experts)
    back = lax.all_to_all(send, "expert", split_axis=0, concat_axis=0, tiled=True)

    def swap(part, mask):
        return lax.ppermute(part, "dp", [(i, i ^ mask) for i in range(groups)])

    total = keep + swap(other, 2).astype(F32)
    sent = total.astype(BF)
    total = total[0] + (swap(sent[1], 8).astype(F32) + swap(sent[2], 4).astype(F32) + swap(sent[3], 12).astype(F32))
    mixed, input_grad, grad_wide, grad_narrow = combine(back, table, total[0], swap(total[1], 1), 3 * rank, inner)
    grad_wide = grad_wide.reshape(1, 3, rank, width // groups)
    grad_narrow = grad_narrow.reshape(1, 3, 1, inner)
    return mixed, input_grad, grad_wide, grad_narrow


def solution(mesh):
    rows = P(("dp", "expert"), None)
    weight = P("expert", None, None)
    return jax.shard_map(
        shards,
        mesh=mesh,
        in_specs=(rows,) * 3 + (weight,) * 12 + (rows,),
        out_specs=(rows, rows, P("expert", None, None, "dp"), P("expert", None, "dp", None)),
        check_vma=False,
    )
```
